256 devices in a mesh: wet: 32 (over x, y, core), trc: 8 (over z).
Axes of the slice: x: 4, y: 4, z: 8, core: 2. Of those that a mesh axis runs over, the one named last changes fastest.
Arguments:
- state_guess: float32 [1024, 32, 128], P('wet', 'trc'), may hold values from -8 to 8
- forcing: float32 [1024, 32, 128], P('wet', 'trc'), may hold values from -4 to 4
- rate: float32 [1024, 32, 128], P('wet', 'trc'), may hold values from 0.02 to 0.3
- explicit: bfloat16 [1024, 8, 128, 128], P('wet', 'trc'), may hold values from -1 to 1.2
- implicit: bfloat16 [1024, 128, 128], P('wet', 'trc'), may hold values from -1 to 1
- col_index: int32 [1024, 8], P('wet'), may hold values from 0 to 1023, as said below
- counts: int32 [1024], P('wet'), may hold values from 3 to 8
Outputs:
- new_state: float32 [1024, 32, 128], P('wet', 'trc')
The draws below stay inside these ranges and needn't reach their ends.
Inputs may be any that keep to these rules, and one draw needn't show every extreme that they name: `col_index`: slot 0 names the row block itself; every slot names a row block within 32 blocks of its own, counted cyclically.
All inputs are finite; a program needn't handle non-finite values.
Results may differ from the reference program's by a relative error of at most 0.0054.
The reference program's roundings to bfloat16 on the way count: a program that leaves them out, or rounds other values in their place, can miss the bound.
Values may be sent and summed in bfloat16 or wider, within the bound.
No kernel may reach another device: no remote copies, remote signals or barrier semaphores. Data moves between devices by JAX's collectives and lax.ppermute only.
A program may use at most 64 MiB of HBM per device.

```python
import math
import jax
import jax.numpy as jnp
from jax import lax

BLOCK = 128
TRACERS = 32
NNZ = 8
STEPS = 4
RB_DEV = 32
TOTAL_RB = 1024


def noise_block(key, shape):
    return jnp.clip(jax.random.normal(key, shape, jnp.float32), -4.0, 4.0)


def row_ramp(shape, low, high):
    rows = lax.broadcasted_iota(jnp.int32, shape, 0).astype(jnp.float32)
    share = rows / max(TOTAL_RB - 1, 1)
    return low * jnp.exp(share * jnp.log(high / low))


def draw_state_guess(key, part):
    key = jax.random.fold_in(key, 41)
    shape = (TOTAL_RB, TRACERS, BLOCK)
    values = jnp.clip(jax.random.normal(key, shape, jnp.float32), -4.0, 4.0) * row_ramp(shape, 0.5, 2.0)
    return values.astype(jnp.float32)


def draw_forcing(key, part):
    key = jax.random.fold_in(key, 53)
    shape = (TOTAL_RB, TRACERS, BLOCK)
    values = jnp.clip(jax.random.normal(key, shape, jnp.float32), -4.0, 4.0) * row_ramp(shape, 0.25, 1.0)
    return values.astype(jnp.float32)


def draw_explicit(key, part):
    key = jax.random.fold_in(key, 11)
    noise_key = jax.random.fold_in(key, 1)
    level_key = jax.random.fold_in(key, 2)
    shape = (TOTAL_RB, NNZ, BLOCK, BLOCK)
    slot_ids = lax.broadcasted_iota(jnp.int32, shape, 1)
    rows = lax.broadcasted_iota(jnp.int32, shape, 2)
    cols = lax.broadcasted_iota(jnp.int32, shape, 3)
    own_scale = 0.18 / BLOCK ** 0.5
    other_scale = 0.2 / (BLOCK * (NNZ - 1)) ** 0.5
    values = noise_block(noise_key, shape) * jnp.where(slot_ids == 0, own_scale, other_scale)
    levels = jax.random.uniform(level_key, (TOTAL_RB, 1, BLOCK, 1), jnp.float32, 0.86, 0.96)
    diagonal = jnp.where((slot_ids == 0) & (rows == cols), levels, 0.0)
    return (values + diagonal).astype(jnp.bfloat16)


def draw_implicit(key, part):
    key = jax.random.fold_in(key, 23)
    noise_key = jax.random.fold_in(key, 1)
    level_key = jax.random.fold_in(key, 2)
    shape = (TOTAL_RB, BLOCK, BLOCK)
    values = noise_block(noise_key, shape) * (0.16 / BLOCK ** 0.5)
    rows = lax.broadcasted_iota(jnp.int32, shape, 1)
    cols = lax.broadcasted_iota(jnp.int32, shape, 2)
    levels = jax.random.uniform(level_key, (TOTAL_RB, BLOCK, 1), jnp.float32, 0.78, 0.88)
    return (values + jnp.where(rows == cols, levels, 0.0)).astype(jnp.bfloat16)


def draw_col_index(key, part):
    key = jax.random.fold_in(key, 37)
    offsets = jax.random.randint(key, (TOTAL_RB, NNZ), -RB_DEV, RB_DEV + 1, jnp.int32)
    slot_ids = lax.broadcasted_iota(jnp.int32, (TOTAL_RB, NNZ), 1)
    offsets = jnp.where(slot_ids == 0, 0, offsets)
    own_rows = lax.broadcasted_iota(jnp.int32, (TOTAL_RB, NNZ), 0)
    return jnp.mod(own_rows + offsets + TOTAL_RB, TOTAL_RB).astype(jnp.int32)


def plant(result, key, smallest, high):
    index_at = [jax.random.randint(jax.random.fold_in(key, axis), (), 0, length) for axis, length in enumerate(result.shape)]
    main_axis = result.shape.index(max(result.shape))
    next_to = index_at[:main_axis] + [(index_at[main_axis] + 1) % result.shape[main_axis]] + index_at[main_axis + 1:]
    return result.at[tuple(index_at)].set(smallest).at[tuple(next_to)].set(high)


def block_scale(key, shape, split, low, largest):
    loudness, own = 1.0, jax.random.fold_in(key, 6)
    for position, shards_of in split:
        steps = jnp.exp(jax.random.uniform(jax.random.fold_in(own, position), (shards_of,), jnp.float32, low / len(split), largest / len(split)))
        loudness = loudness * jnp.repeat(steps, shape[position] // shards_of).reshape([-1 if axis == position else 1 for axis in range(len(shape))])
    return loudness


def setup_inputs(seed: int = 0) -> dict:
    keys = jax.random.split(jax.random.key(seed), 8)
    state_guess = draw_state_guess(jax.random.fold_in(keys[7], 71), 0)
    forcing = draw_forcing(jax.random.fold_in(keys[7], 71), 0)
    rate = jnp.clip(jnp.exp(math.log(0.3) - 2.7080503 * jax.random.uniform(keys[2], (TOTAL_RB, TRACERS, BLOCK), jnp.float32) ** block_scale(keys[2], (TOTAL_RB, TRACERS, BLOCK), ((0, 32), (1, 8)), -0.2, 0.2)), 0.02, 0.3)
    explicit = draw_explicit(jax.random.fold_in(keys[7], 71), 0)
    implicit = draw_implicit(jax.random.fold_in(keys[7], 71), 0)
    col_index = draw_col_index(jax.random.fold_in(keys[7], 71), 0)
    counts = plant(jax.random.randint(keys[6], (TOTAL_RB,), 3, NNZ + 1), jax.random.fold_in(keys[6], 1), 3, NNZ).astype(jnp.int32)
    return dict(state_guess=state_guess, forcing=forcing, rate=rate, explicit=explicit, implicit=implicit, col_index=col_index, counts=counts)


def cycle(field, source, rate, explicit, implicit, col_index, live_mask):
    inverse = implicit.astype(jnp.float32)
    for substep in range(STEPS):
        rounded = field.astype(jnp.bfloat16)

        def one_row(pieces):
            blocks, indices, mask_row = pieces
            picked = jnp.take(rounded, indices, axis=0) * mask_row[:, None, None]
            return jnp.einsum('stk,sik->ti', picked.astype(jnp.float32), blocks.astype(jnp.float32))
        moved = lax.map(one_row, (explicit, col_index, live_mask))
        mixed = (moved - rate * field + source).astype(jnp.bfloat16)
        field = jnp.einsum('btk,bik->bti', mixed.astype(jnp.float32), inverse)
    return field

def reference(state_guess, forcing, rate, explicit, implicit, col_index, counts):
    slot_ids = lax.broadcasted_iota(jnp.int32, col_index.shape, 1)
    live_mask = (slot_ids < counts[:, None]).astype(jnp.bfloat16)
    zero_source = jnp.zeros_like(forcing)

    def apply_jac(vector):
        return cycle(vector, zero_source, rate, explicit, implicit, col_index, live_mask) - vector
    start = state_guess - cycle(state_guess, forcing, rate, explicit, implicit, col_index, live_mask)
    norm_zero = jnp.sqrt(jnp.sum(start * start))
    basis_one = start / norm_zero
    krylov = apply_jac(basis_one)
    coef_aa = jnp.sum(basis_one * krylov)
    krylov = krylov - coef_aa * basis_one
    coef_ba = jnp.sqrt(jnp.sum(krylov * krylov))
    basis_two = krylov / coef_ba
    krylov = apply_jac(basis_two)
    coef_ab = jnp.sum(basis_one * krylov)
    coef_bb = jnp.sum(basis_two * krylov)
    krylov = krylov - coef_ab * basis_one - coef_bb * basis_two
    coef_cb = jnp.sqrt(jnp.sum(krylov * krylov))
    gram_aa = coef_aa * coef_aa + coef_ba * coef_ba
    gram_ab = coef_aa * coef_ab + coef_ba * coef_bb
    gram_bb = coef_ab * coef_ab + coef_bb * coef_bb + coef_cb * coef_cb
    right_one = norm_zero * coef_aa
    right_two = norm_zero * coef_ab
    determinant = gram_aa * gram_bb - gram_ab * gram_ab
    weight_one = (gram_bb * right_one - gram_ab * right_two) / determinant
    weight_two = (gram_aa * right_two - gram_ab * right_one) / determinant
    return state_guess + weight_one * basis_one + weight_two * basis_two
```

```python
import functools
import jax
import jax.numpy as jnp
from jax import lax
from jax.experimental import pallas as pl
from jax.experimental.pallas import tpu as pltpu
from jax.sharding import PartitionSpec as P

STEPS = 4
LEAD = 8
MIB = 1024 * 1024
NN = (((1,), (0,)), ((), ()))
VMEM = pl.BlockSpec(memory_space=pltpu.VMEM)
SMEM = pl.BlockSpec(memory_space=pltpu.SMEM)


def turn_kernel(gathered, turned, buffers, sems):
    rows, slots, _, block = gathered.shape
    copies = [pltpu.make_async_copy(gathered.at[b], buffers.at[b % 4], sems.at[b % 4]) for b in range(rows)]
    for b in range(3):
        copies[b].start()
    for b in range(rows):
        copies[b].wait()
        if b + 3 < rows:
            copies[b + 3].start()
        held = buffers.at[b % 4]
        for s in range(slots):
            turned[b, s * block : (s + 1) * block, :] = held[s, :block, :].T
        inverse = jnp.concatenate([held[s, block:, :] for s in range(slots)], axis=0)
        turned[b, slots * block :, :] = inverse.T


def turn(gathered):
    rows, slots, height, block = gathered.shape
    return pl.pallas_call(
        turn_kernel,
        out_shape=pltpu.VMEM((rows, (slots + 1) * block, block), gathered.dtype),
        in_specs=[pl.BlockSpec(memory_space=pl.ANY)],
        out_specs=VMEM,
        scratch_shapes=[pltpu.VMEM((4, slots, height, block), gathered.dtype), pltpu.SemaphoreType.DMA((4,))],
        compiler_params=pltpu.CompilerParams(vmem_limit_bytes=16 * MIB),
    )(gathered)


def step_kernel(mode, has_source, group, *refs):
    refs = list(refs)
    places, own, before, after, field, rate = refs[:6]
    del refs[:6]
    source = refs.pop(0) if has_source else None
    matrix = refs.pop(0)
    extra = {"plain": 0, "start": 1, "dots": 2}[mode]
    held, refs = refs[:extra], refs[extra:]
    ext = refs.pop()
    rows, slots = places.shape
    block = field.shape[1]
    tracers = field.shape[0] // rows
    pair = 2 * tracers
    size = field.shape[0]
    for i, part in enumerate((before, own, after)):
        ext[LEAD + i * size : LEAD + (i + 1) * size, :] = part[...].astype(jnp.float32)
    ext[LEAD + 3 * size : LEAD + 3 * size + pair, :] = jnp.zeros((pair, block), jnp.float32)
    upper = lax.broadcasted_iota(jnp.int32, (pair, block), 0) < tracers
    sums = [jnp.zeros((pair, block), jnp.float32) for _ in range(5)]
    for first in range(0, rows, group):
        mixed = []
        for b in range(first, first + group, 2):
            parts = []
            for s in range(slots):
                high = ext[pl.ds(places[b, s], pair), :]
                low = ext[pl.ds(places[b + 1, s] - tracers, pair), :]
                parts.append(jnp.where(upper, high, low).astype(jnp.bfloat16))
            picked = jnp.concatenate(parts, axis=1)
            weights = jnp.concatenate([matrix[b, : slots * block, :], matrix[b + 1, : slots * block, :]], axis=1)
            both = lax.dot_general(picked, weights, NN, preferred_element_type=jnp.float32)
            moved = jnp.where(upper, both[:, :block], both[:, block:])
            here = slice(b * tracers, b * tracers + pair)
            value = moved - rate[here, :] * field[here, :]
            if has_source:
                value = value + source[here, :]
            mixed.append(value.astype(jnp.bfloat16))
        for b, value in zip(range(first, first + group, 2), mixed):
            weights = jnp.concatenate([matrix[b, slots * block :, :], matrix[b + 1, slots * block :, :]], axis=1)
            both = lax.dot_general(value, weights, NN, preferred_element_type=jnp.float32)
            new = jnp.where(upper, both[:, :block], both[:, block:])
            here = slice(b * tracers, b * tracers + pair)
            if mode == "dots":
                base, image = held[0][here, :], held[1][here, :]
                one, two = image - base, new - image
                terms = (one * one, one * two, two * two, base * one, base * two)
                sums = [total + term for total, term in zip(sums, terms)]
            else:
                if mode == "start":
                    new = held[0][here, :] - new
                refs[0][here, :] = new
                refs[1][here, :] = new.astype(jnp.bfloat16)
    if mode == "dots":
        for i, total in enumerate(sums):
            refs[0][i : i + 1, :] = jnp.sum(total, axis=0, keepdims=True)
        refs[0][5:8, :] = jnp.zeros((3, block), jnp.float32)


def step(mode, places, own, before, after, field, rate, source, matrix, *held):
    size, block = field.shape
    args = [places, own, before, after, field, rate] + ([] if source is None else [source]) + [matrix, *held]
    if mode == "dots":
        out_shape = jax.ShapeDtypeStruct((8, block), jnp.float32)
    else:
        out_shape = tuple(jax.ShapeDtypeStruct(field.shape, t) for t in (jnp.float32, jnp.bfloat16))
    return pl.pallas_call(
        functools.partial(step_kernel, mode, source is not None, 16),
        out_shape=out_shape,
        in_specs=[SMEM] + [VMEM] * (len(args) - 1),
        out_specs=VMEM if mode == "dots" else (VMEM, VMEM),
        scratch_shapes=[pltpu.VMEM((LEAD + 3 * size + 8, block), jnp.float32)],
        compiler_params=pltpu.CompilerParams(vmem_limit_bytes=24 * MIB),
    )(*args)


def finish_kernel(dots, state, base, image, out):
    def entry(i):
        return jnp.sum(dots[i : i + 1, :], axis=1, keepdims=True)

    gram_aa, gram_ab, gram_bb, right_one, right_two = (entry(i) for i in range(5))
    determinant = gram_aa * gram_bb - gram_ab * gram_ab
    weight_one = (gram_bb * right_one - gram_ab * right_two) / determinant
    weight_two = (gram_aa * right_two - gram_ab * right_one) / determinant
    out[...] = state[...] + weight_one * base[...] + weight_two * image[...]


def body(state_guess, forcing, rate, explicit, implicit, col_index, counts):
    rows, tracers, block = state_guess.shape
    wet, trc = lax.axis_size("wet"), lax.axis_size("trc")
    start_row = lax.axis_index("wet") * rows
    positions = jnp.mod(col_index - start_row + rows + wet * rows, wet * rows)
    live = lax.broadcasted_iota(jnp.int32, col_index.shape, 1) < counts[:, None]
    places = LEAD + tracers * jnp.where(live, positions, 3 * rows)
    merged = jnp.concatenate([explicit, implicit[:, None]], axis=2)
    matrix = turn(lax.all_gather(merged, "trc", axis=1, tiled=True))
    up = [(i, (i + 1) % wet) for i in range(wet)]
    down = [(j, i) for i, j in up]
    flat = (rows * tracers, block)
    state, source, rates = (jnp.reshape(a, flat) for a in (state_guess, forcing, rate))

    def run(mode, field, rounded, source, *held):
        for substep in range(STEPS):
            before = lax.ppermute(rounded, "wet", up)
            after = lax.ppermute(rounded, "wet", down)
            last = substep == STEPS - 1
            new = step(mode if last else "plain", places, rounded, before, after, field, rates, source, matrix, *(held if last else ()))
            if not (last and mode == "dots"):
                field, rounded = new
        return new

    base, base16 = run("start", state, state.astype(jnp.bfloat16), source, state)
    image, image16 = run("plain", base, base16, None)
    dots = run("dots", image, image16, None, base, image)
    distance = 1
    while distance < wet:
        dots = dots + lax.ppermute(dots, "wet", [(i, i ^ distance) for i in range(wet)])
        distance *= 2
    distance = 1
    while distance < trc:
        dots = dots + lax.ppermute(dots, "trc", [(i, i ^ distance) for i in range(trc)])
        distance *= 2
    out = pl.pallas_call(
        finish_kernel,
        out_shape=jax.ShapeDtypeStruct(flat, jnp.float32),
        in_specs=[VMEM] * 4,
        out_specs=VMEM,
    )(dots, state, base, image)
    return jnp.reshape(out, state_guess.shape)


def solution(mesh):
    return jax.shard_map(
        body,
        mesh=mesh,
        in_specs=(
            P("wet", "trc", None),
            P("wet", "trc", None),
            P("wet", "trc", None),
            P("wet", "trc", None, None),
            P("wet", "trc", None),
            P("wet", None),
            P("wet"),
        ),
        out_specs=P("wet", "trc", None),
        check_vma=False,
    )
```

```python
import functools
import jax
import jax.numpy as jnp
from jax import lax
from jax.experimental import pallas as pl
from jax.experimental.pallas import tpu as pltpu
from jax.sharding import PartitionSpec as P

STEPS = 4
LEAD = 8
MIB = 1024 * 1024
NN = (((1,), (0,)), ((), ()))
VMEM = pl.BlockSpec(memory_space=pltpu.VMEM)
SMEM = pl.BlockSpec(memory_space=pltpu.SMEM)


def turn_kernel(count, *refs):
    pieces, turned = refs[:-1], refs[-1]
    block = turned.shape[2]
    row = 0
    for first in range(0, len(pieces), count):
        half = pieces[first].shape[0]
        for i in range(half):
            for j in range(count):
                turned[row + i, j * block : (j + 1) * block, :] = pieces[first + j][i, :block, :].T
        row += half


def turn(count, pieces):
    block = pieces[0].shape[2]
    rows = sum(p.shape[0] for p in pieces) // count
    return pl.pallas_call(
        functools.partial(turn_kernel, count),
        out_shape=pltpu.VMEM((rows, count * block, block), pieces[0].dtype),
        in_specs=[VMEM] * len(pieces),
        out_specs=VMEM,
        compiler_params=pltpu.CompilerParams(vmem_limit_bytes=16 * MIB),
    )(*pieces)


def turn_inverse_kernel(offsets, trc, *refs):
    pieces, (turned, held, sems) = refs[:-3], refs[-3:]
    me = lax.axis_index("trc")
    rows, block = turned.shape[0], turned.shape[1]
    half = rows // 2
    slab = block // trc
    copies = []
    for i, (offset, piece) in enumerate(zip(offsets, pieces)):
        place = pl.ds(pl.multiple_of(slab * lax.rem(me + offset, trc), slab), slab)
        low = i % 2 * half
        copies.append(pltpu.make_async_copy(piece.at[:, block:, :], held.at[low : low + half, place, :], sems.at[i]))
    for copy in copies:
        copy.start()
    for copy in copies:
        copy.wait()
    for b in range(rows):
        turned[b] = held[b].T


def turn_inverse(offsets, pieces, trc):
    half, height, block = pieces[0].shape
    shape = (2 * half, block, block)
    return pl.pallas_call(
        functools.partial(turn_inverse_kernel, [o for o in offsets for _ in range(2)], trc),
        out_shape=pltpu.VMEM(shape, pieces[0].dtype),
        in_specs=[pl.BlockSpec(memory_space=pl.ANY)] * len(pieces),
        out_specs=VMEM,
        scratch_shapes=[pltpu.VMEM(shape, pieces[0].dtype), pltpu.SemaphoreType.DMA((len(pieces),))],
        compiler_params=pltpu.CompilerParams(vmem_limit_bytes=16 * MIB),
    )(*pieces)


def ring(low, high):
    trc = lax.axis_size("trc")
    up = [(i, (i + 1) % trc) for i in range(trc)]
    down = [(j, i) for i, j in up]
    shards = {0: (low, high)}
    parts = [turn(1, [low, high])]
    offsets = [0]
    before, after = (low, high), (low, high)
    for distance in range(1, (trc - 1) // 2 + 1):
        before = tuple(lax.ppermute(p, "trc", up) for p in before)
        after = tuple(lax.ppermute(p, "trc", down) for p in after)
        shards[trc - distance], shards[distance] = before, after
        parts.append(turn(2, [before[0], after[0], before[1], after[1]]))
        offsets += [trc - distance, distance]
    if trc % 2 == 0:
        last = (lax.ppermute(before[0], "trc", up), lax.ppermute(after[1], "trc", down))
        shards[trc // 2] = last
        parts.insert(1, turn(1, list(last)))
        offsets.insert(1, trc // 2)
    pieces = [piece for offset in offsets for piece in shards[offset]]
    return offsets, parts, turn_inverse(offsets, pieces, trc)


def step_kernel(mode, has_source, parts, group, *refs):
    refs = list(refs)
    places, own, before, after, field, rate = refs[:6]
    del refs[:6]
    source = refs.pop(0) if has_source else None
    matrix = [refs.pop(0) for _ in range(parts)]
    inverse = refs.pop(0)
    extra = {"plain": 0, "start": 1, "dots": 2}[mode]
    held, refs = refs[:extra], refs[extra:]
    ext = refs.pop()
    rows, slots = places.shape
    block = field.shape[1]
    tracers = field.shape[0] // rows
    pair = 2 * tracers
    size = field.shape[0]
    for i, part in enumerate((before, own, after)):
        ext[LEAD + i * size : LEAD + (i + 1) * size, :] = part[...].astype(jnp.float32)
    ext[LEAD + 3 * size : LEAD + 3 * size + pair, :] = jnp.zeros((pair, block), jnp.float32)
    upper = lax.broadcasted_iota(jnp.int32, (pair, block), 0) < tracers
    sums = [jnp.zeros((pair, block), jnp.float32) for _ in range(5)]
    for first in range(0, rows, group):
        mixed = []
        for b in range(first, first + group, 2):
            chosen = []
            for s in range(slots):
                high = ext[pl.ds(places[b, s], pair), :]
                low = ext[pl.ds(places[b + 1, s] - tracers, pair), :]
                chosen.append(jnp.where(upper, high, low).astype(jnp.bfloat16))
            picked = jnp.concatenate(chosen, axis=1)
            weights = jnp.concatenate([jnp.concatenate([part[i] for part in matrix], axis=0) for i in (b, b + 1)], axis=1)
            both = lax.dot_general(picked, weights, NN, preferred_element_type=jnp.float32)
            moved = jnp.where(upper, both[:, :block], both[:, block:])
            here = slice(b * tracers, b * tracers + pair)
            value = moved - rate[here, :] * field[here, :]
            if has_source:
                value = value + source[here, :]
            mixed.append(value.astype(jnp.bfloat16))
        for b, value in zip(range(first, first + group, 2), mixed):
            weights = jnp.concatenate([inverse[b], inverse[b + 1]], axis=1)
            both = lax.dot_general(value, weights, NN, preferred_element_type=jnp.float32)
            new = jnp.where(upper, both[:, :block], both[:, block:])
            here = slice(b * tracers, b * tracers + pair)
            if mode == "dots":
                base, image = held[0][here, :], held[1][here, :]
                one, two = image - base, new - image
                terms = (one * one, one * two, two * two, base * one, base * two)
                sums = [total + term for total, term in zip(sums, terms)]
            else:
                if mode == "start":
                    new = held[0][here, :] - new
                refs[0][here, :] = new
                refs[1][here, :] = new.astype(jnp.bfloat16)
    if mode == "dots":
        lane = lax.broadcasted_iota(jnp.int32, (1, block), 1)
        row = jnp.zeros((1, block), jnp.float32)
        for i, total in enumerate(sums):
            row = jnp.where(lane == i, jnp.sum(total, keepdims=True), row)
        refs[0][...] = jnp.broadcast_to(row[None], refs[0].shape)


def step(mode, peers, places, own, before, after, field, rate, source, matrix, *held):
    size, block = field.shape
    args = [places, own, before, after, field, rate] + ([] if source is None else [source]) + [*matrix, *held]
    if mode == "dots":
        out_shape = jax.ShapeDtypeStruct((peers, 1, block), jnp.float32)
    else:
        out_shape = tuple(jax.ShapeDtypeStruct(field.shape, t) for t in (jnp.float32, jnp.bfloat16))
    return pl.pallas_call(
        functools.partial(step_kernel, mode, source is not None, len(matrix) - 1, 16),
        out_shape=out_shape,
        in_specs=[SMEM] + [VMEM] * (len(args) - 1),
        out_specs=VMEM if mode == "dots" else (VMEM, VMEM),
        scratch_shapes=[pltpu.VMEM((LEAD + 3 * size + 8, block), jnp.float32)],
        compiler_params=pltpu.CompilerParams(vmem_limit_bytes=24 * MIB),
    )(*args)


def finish_kernel(dots, state, base, image, out):
    row = jnp.sum(dots[...], axis=0)

    def entry(i):
        return row[:, i : i + 1]

    gram_aa, gram_ab, gram_bb, right_one, right_two = (entry(i) for i in range(5))
    determinant = gram_aa * gram_bb - gram_ab * gram_ab
    weight_one = (gram_bb * right_one - gram_ab * right_two) / determinant
    weight_two = (gram_aa * right_two - gram_ab * right_one) / determinant
    out[...] = state[...] + weight_one * base[...] + weight_two * image[...]


def body(state_guess, forcing, rate, explicit, implicit, col_index, counts):
    rows, tracers, block = state_guess.shape
    wet, trc = lax.axis_size("wet"), lax.axis_size("trc")
    start_row = lax.axis_index("wet") * rows
    positions = jnp.mod(col_index - start_row + rows + wet * rows, wet * rows)
    live = lax.broadcasted_iota(jnp.int32, col_index.shape, 1) < counts[:, None]
    places = LEAD + tracers * jnp.where(live, positions, 3 * rows)
    half = rows // 2
    low, high = (jnp.concatenate([explicit[i : i + half, 0], implicit[i : i + half]], axis=1) for i in (0, half))
    offsets, parts, inverse = ring(low, high)
    matrix = (*parts, inverse)
    slot_order = jnp.mod(lax.axis_index("trc") + jnp.array(offsets, jnp.int32), trc)
    named = lax.broadcasted_iota(jnp.int32, (rows, trc, trc), 2) == slot_order[None, :, None]
    places = jnp.sum(jnp.where(named, places[:, None, :], 0), axis=2)
    up = [(i, (i + 1) % wet) for i in range(wet)]
    down = [(j, i) for i, j in up]
    flat = (rows * tracers, block)
    state, source, rates = (jnp.reshape(a, flat) for a in (state_guess, forcing, rate))

    def run(mode, field, rounded, source, *held):
        for substep in range(STEPS):
            before = lax.ppermute(rounded, "wet", up)
            after = lax.ppermute(rounded, "wet", down)
            last = substep == STEPS - 1
            new = step(mode if last else "plain", wet * trc, places, rounded, before, after, field, rates, source, matrix, *(held if last else ()))
            if not (last and mode == "dots"):
                field, rounded = new
        return new

    base, base16 = run("start", state, state.astype(jnp.bfloat16), source, state)
    image, image16 = run("plain", base, base16, None)
    dots = run("dots", image, image16, None, base, image)
    dots = lax.all_to_all(dots, ("wet", "trc"), 0, 0)
    out = pl.pallas_call(
        finish_kernel,
        out_shape=jax.ShapeDtypeStruct(flat, jnp.float32),
        in_specs=[VMEM] * 4,
        out_specs=VMEM,
    )(dots, state, base, image)
    return jnp.reshape(out, state_guess.shape)


def solution(mesh):
    return jax.shard_map(
        body,
        mesh=mesh,
        in_specs=(
            P("wet", "trc", None),
            P("wet", "trc", None),
            P("wet", "trc", None),
            P("wet", "trc", None, None),
            P("wet", "trc", None),
            P("wet", None),
            P("wet"),
        ),
        out_specs=P("wet", "trc", None),
        check_vma=False,
    )
```

```python
import functools
import jax
import jax.numpy as jnp
from jax import lax
from jax.experimental import pallas as pl
from jax.experimental.pallas import tpu as pltpu
from jax.sharding import PartitionSpec as P

STEPS = 4
LEAD = 8
MIB = 1024 * 1024
NN = (((1,), (0,)), ((), ()))
VMEM = pl.BlockSpec(memory_space=pltpu.VMEM)
SMEM = pl.BlockSpec(memory_space=pltpu.SMEM)
CHUNKS = 4
WALK = ((0, 0), (0, 1), (0, 2), (0, 3), (1, 3), (1, 2), (1, 1), (2, 1), (2, 2), (2, 3), (3, 3), (3, 2), (3, 1), (3, 0), (2, 0), (1, 0))


def walk_order(wet):
    if wet != 32:
        return list(range(wet))
    return [(4 * x + y) * 2 + core for x, y in WALK for core in range(2)]


def turn_kernel(count, *refs):
    pieces, turned = refs[:-1], refs[-1]
    block = turned.shape[2]
    row = 0
    for first in range(0, len(pieces), count):
        half = pieces[first].shape[0]
        for i in range(half):
            for j in range(count):
                turned[row + i, j * block : (j + 1) * block, :] = pieces[first + j][i, :block, :].T
        row += half


def turn(count, pieces):
    block = pieces[0].shape[2]
    rows = sum(p.shape[0] for p in pieces) // count
    return pl.pallas_call(
        functools.partial(turn_kernel, count),
        out_shape=pltpu.VMEM((rows, count * block, block), pieces[0].dtype),
        in_specs=[VMEM] * len(pieces),
        out_specs=VMEM,
        compiler_params=pltpu.CompilerParams(vmem_limit_bytes=16 * MIB),
    )(*pieces)


def turn_inverse_kernel(offsets, trc, *refs):
    pieces, (turned, held, sems) = refs[:-3], refs[-3:]
    me = lax.axis_index("trc")
    rows, block = turned.shape[0], turned.shape[1]
    height = pieces[0].shape[0]
    slab = block // trc
    copies = []
    for i, (offset, piece) in enumerate(zip(offsets, pieces)):
        place = pl.ds(pl.multiple_of(slab * lax.rem(me + offset, trc), slab), slab)
        low = i * height % rows
        copies.append(pltpu.make_async_copy(piece.at[:, block:, :], held.at[low : low + height, place, :], sems.at[i]))
    for copy in copies:
        copy.start()
    for copy in copies:
        copy.wait()
    for b in range(rows):
        turned[b] = held[b].T


def turn_inverse(offsets, pieces, trc):
    chunks = len(pieces) // len(offsets)
    shape = (chunks * pieces[0].shape[0], pieces[0].shape[2], pieces[0].shape[2])
    return pl.pallas_call(
        functools.partial(turn_inverse_kernel, [o for o in offsets for _ in range(chunks)], trc),
        out_shape=pltpu.VMEM(shape, pieces[0].dtype),
        in_specs=[pl.BlockSpec(memory_space=pl.ANY)] * len(pieces),
        out_specs=VMEM,
        scratch_shapes=[pltpu.VMEM(shape, pieces[0].dtype), pltpu.SemaphoreType.DMA((len(pieces),))],
        compiler_params=pltpu.CompilerParams(vmem_limit_bytes=16 * MIB),
    )(*pieces)


def ring(chunks):
    trc = lax.axis_size("trc")
    up = [(i, (i + 1) % trc) for i in range(trc)]
    down = [(j, i) for i, j in up]
    shards = {0: chunks}
    parts = [turn(1, chunks)]
    offsets = [0]
    before, after = chunks, chunks
    for distance in range(1, (trc - 1) // 2 + 1):
        before = [lax.ppermute(p, "trc", up) for p in before]
        after = [lax.ppermute(p, "trc", down) for p in after]
        shards[trc - distance], shards[distance] = before, after
        parts.append(turn(2, [p for both in zip(before, after) for p in both]))
        offsets += [trc - distance, distance]
    if trc % 2 == 0:
        middle = len(chunks) // 2
        last = [lax.ppermute(p, "trc", up) for p in before[:middle]] + [lax.ppermute(p, "trc", down) for p in after[middle:]]
        shards[trc // 2] = last
        parts.insert(1, turn(1, last))
        offsets.insert(1, trc // 2)
    pieces = [piece for offset in offsets for piece in shards[offset]]
    return offsets, parts, turn_inverse(offsets, pieces, trc)


def scalars_kernel(places, out):
    for b in range(places.shape[0]):
        for s in range(places.shape[1]):
            out[b, s] = places[b, s]


def scalars(places):
    return pl.pallas_call(scalars_kernel, out_shape=pltpu.SMEM(places.shape, places.dtype), in_specs=[SMEM], out_specs=SMEM)(places)


def step_kernel(mode, has_source, parts, group, *refs):
    refs = list(refs)
    places, own, before, after, field, rate = refs[:6]
    del refs[:6]
    source = refs.pop(0) if has_source else None
    matrix = [refs.pop(0) for _ in range(parts)]
    inverse = refs.pop(0)
    extra = {"plain": 0, "start": 1, "dots": 2}[mode]
    held, refs = refs[:extra], refs[extra:]
    ext = refs.pop()
    rows, slots = places.shape
    block = field.shape[1]
    tracers = field.shape[0] // rows
    pair = 2 * tracers
    size = field.shape[0]
    for i, part in enumerate((before, own, after)):
        ext[LEAD + i * size : LEAD + (i + 1) * size, :] = part[...].astype(jnp.float32)
    ext[LEAD + 3 * size : LEAD + 3 * size + pair, :] = jnp.zeros((pair, block), jnp.float32)
    upper = lax.broadcasted_iota(jnp.int32, (pair, block), 0) < tracers
    sums = [jnp.zeros((pair, block), jnp.float32) for _ in range(5)]
    for first in range(0, rows, group):
        mixed = []
        for b in range(first, first + group, 2):
            chosen = []
            for s in range(slots):
                high = ext[pl.ds(places[b, s], pair), :]
                low = ext[pl.ds(places[b + 1, s] - tracers, pair), :]
                chosen.append(jnp.where(upper, high, low).astype(jnp.bfloat16))
            picked = jnp.concatenate(chosen, axis=1)
            weights = jnp.concatenate([jnp.concatenate([part[i] for part in matrix], axis=0) for i in (b, b + 1)], axis=1)
            both = lax.dot_general(picked, weights, NN, preferred_element_type=jnp.float32)
            moved = jnp.where(upper, both[:, :block], both[:, block:])
            here = slice(b * tracers, b * tracers + pair)
            value = moved - rate[here, :] * field[here, :]
            if has_source:
                value = value + source[here, :]
            mixed.append(value.astype(jnp.bfloat16))
        for b, value in zip(range(first, first + group, 2), mixed):
            weights = jnp.concatenate([inverse[b], inverse[b + 1]], axis=1)
            both = lax.dot_general(value, weights, NN, preferred_element_type=jnp.float32)
            new = jnp.where(upper, both[:, :block], both[:, block:])
            here = slice(b * tracers, b * tracers + pair)
            if mode == "dots":
                base, image = held[0][here, :], held[1][here, :]
                one, two = image - base, new - image
                terms = (one * one, one * two, two * two, base * one, base * two)
                sums = [total + term for total, term in zip(sums, terms)]
            else:
                if mode == "start":
                    new = held[0][here, :] - new
                refs[0][here, :] = new
                refs[1][here, :] = new.astype(jnp.bfloat16)
    if mode == "dots":
        lane = lax.broadcasted_iota(jnp.int32, (1, block), 1)
        row = jnp.zeros((1, block), jnp.float32)
        for i, total in enumerate(sums):
            row = jnp.where(lane == i, jnp.sum(total, keepdims=True), row)
        refs[0][...] = jnp.broadcast_to(row[None], refs[0].shape)


def step(mode, peers, places, own, before, after, field, rate, source, matrix, *held):
    size, block = field.shape
    args = [places, own, before, after, field, rate] + ([] if source is None else [source]) + [*matrix, *held]
    if mode == "dots":
        out_shape = jax.ShapeDtypeStruct((peers, 1, block), jnp.float32)
    else:
        out_shape = tuple(jax.ShapeDtypeStruct(field.shape, t) for t in (jnp.float32, jnp.bfloat16))
    return pl.pallas_call(
        functools.partial(step_kernel, mode, source is not None, len(matrix) - 1, places.shape[0]),
        out_shape=out_shape,
        in_specs=[SMEM] + [VMEM] * (len(args) - 1),
        out_specs=VMEM if mode == "dots" else (VMEM, VMEM),
        scratch_shapes=[pltpu.VMEM((LEAD + 3 * size + 8, block), jnp.float32)],
        compiler_params=pltpu.CompilerParams(vmem_limit_bytes=24 * MIB),
    )(*args)


def finish_kernel(dots, state, base, image, out):
    row = dots[...]

    def entry(i):
        return row[:, i : i + 1]

    gram_aa, gram_ab, gram_bb, right_one, right_two = (entry(i) for i in range(5))
    determinant = gram_aa * gram_bb - gram_ab * gram_ab
    weight_one = (gram_bb * right_one - gram_ab * right_two) / determinant
    weight_two = (gram_aa * right_two - gram_ab * right_one) / determinant
    out[...] = state[...] + weight_one * base[...] + weight_two * image[...]


def body(state_guess, forcing, rate, explicit, implicit, col_index, counts):
    rows, tracers, block = state_guess.shape
    wet, trc = lax.axis_size("wet"), lax.axis_size("trc")
    start_row = lax.axis_index("wet") * rows
    positions = jnp.mod(col_index - start_row + rows + wet * rows, wet * rows)
    live = lax.broadcasted_iota(jnp.int32, col_index.shape, 1) < counts[:, None]
    places = LEAD + tracers * jnp.where(live, positions, 3 * rows)
    order = walk_order(wet)
    there = [(i, place) for i, place in enumerate(order)]
    back = [(place, i) for i, place in there]
    chunk = rows // CHUNKS
    chunks = [jnp.concatenate([explicit[i : i + chunk, 0], implicit[i : i + chunk]], axis=1) for i in range(0, rows, chunk)]
    offsets, parts, inverse = ring([lax.ppermute(p, "wet", there) for p in chunks])
    matrix = (*parts, inverse)
    slot_order = jnp.mod(lax.axis_index("trc") + jnp.array(offsets, jnp.int32), trc)
    named = lax.broadcasted_iota(jnp.int32, (rows, trc, trc), 2) == slot_order[None, :, None]
    places = scalars(lax.ppermute(jnp.sum(jnp.where(named, places[:, None, :], 0), axis=2), "wet", there))
    up = [(order[i], order[(i + 1) % wet]) for i in range(wet)]
    down = [(j, i) for i, j in up]
    flat = (rows * tracers, block)
    home = jnp.reshape(state_guess, flat)
    state, source, rates = (lax.ppermute(jnp.reshape(a, flat), "wet", there) for a in (state_guess, forcing, rate))

    def run(mode, field, rounded, source, *held):
        for substep in range(STEPS):
            before = lax.ppermute(rounded, "wet", up)
            after = lax.ppermute(rounded, "wet", down)
            last = substep == STEPS - 1
            new = step(mode if last else "plain", wet * trc, places, rounded, before, after, field, rates, source, matrix, *(held if last else ()))
            if not (last and mode == "dots"):
                field, rounded = new
        return new

    base, base16 = run("start", state, state.astype(jnp.bfloat16), source, state)
    image, image16 = run("plain", base, base16, None)
    dots = run("dots", image, image16, None, base, image)
    base, image = (lax.ppermute(a, "wet", back) for a in (base, image))
    dots = jnp.sum(lax.all_to_all(dots, ("wet", "trc"), 0, 0), axis=0)
    out = pl.pallas_call(
        finish_kernel,
        out_shape=jax.ShapeDtypeStruct(flat, jnp.float32),
        in_specs=[VMEM] * 4,
        out_specs=VMEM,
    )(dots, home, base, image)
    return jnp.reshape(out, state_guess.shape)


def solution(mesh):
    return jax.shard_map(
        body,
        mesh=mesh,
        in_specs=(
            P("wet", "trc", None),
            P("wet", "trc", None),
            P("wet", "trc", None),
            P("wet", "trc", None, None),
            P("wet", "trc", None),
            P("wet", None),
            P("wet"),
        ),
        out_specs=P("wet", "trc", None),
        check_vma=False,
    )
```

```python
import functools
import jax
import jax.numpy as jnp
from jax import lax
from jax.experimental import pallas as pl
from jax.experimental.pallas import tpu as pltpu
from jax.sharding import PartitionSpec as P

STEPS = 4
LEAD = 8
MIB = 1024 * 1024
NN = (((1,), (0,)), ((), ()))
VMEM = pl.BlockSpec(memory_space=pltpu.VMEM)
SMEM = pl.BlockSpec(memory_space=pltpu.SMEM)
EIGHTHS = (4, 4)
ANY = pl.BlockSpec(memory_space=pl.ANY)
TOKEN = jax.ShapeDtypeStruct((8, 128), jnp.float32)
WALK = ((0, 3), (0, 2), (0, 1), (0, 0), (1, 0), (1, 1), (2, 1), (2, 0), (3, 0), (3, 1), (3, 2), (3, 3), (2, 3), (2, 2), (1, 2), (1, 3))


def walk_order(wet):
    if wet != 32:
        return list(range(wet))
    return [(4 * x + y) * 2 + core for x, y in WALK for core in range(2)]


def turn_pieces(count, pieces, turned):
    block = turned.shape[2]
    row = 0
    for first in range(0, len(pieces), count):
        for j in range(count):
            piece = pieces[first + j]
            for i in range(piece.shape[0]):
                turned[row + i, j * block : (j + 1) * block, :] = piece[i, :block, :].T
        row += piece.shape[0]


def slabs_of(count, pieces, block):
    for j in range(count):
        row = 0
        for piece in pieces[j::count]:
            yield j, row, piece[:, block:, :]
            row += piece.shape[0]


def turn_kernel(count, *refs):
    pieces, (turned, kept, token) = refs[:-3], refs[-3:]
    turn_pieces(count, pieces, turned)
    slab = kept.shape[1] // count
    for j, row, values in slabs_of(count, pieces, turned.shape[2]):
        kept[row : row + values.shape[0], j * slab : (j + 1) * slab, :] = values
    token[...] = jnp.zeros(token.shape, token.dtype)


def turn(count, pieces):
    height, block = pieces[0].shape[1:]
    dtype = pieces[0].dtype
    rows = sum(p.shape[0] for p in pieces) // count
    return pl.pallas_call(
        functools.partial(turn_kernel, count),
        out_shape=(pltpu.VMEM((rows, count * block, block), dtype), pltpu.VMEM((rows, count * (height - block), block), dtype), TOKEN),
        in_specs=[VMEM] * len(pieces),
        out_specs=(VMEM, VMEM, VMEM),
        compiler_params=pltpu.CompilerParams(vmem_limit_bytes=16 * MIB),
    )(*pieces)


def turn_last_kernel(trc, sources, total, *refs):
    pieces, kept, (turned, inverse, held) = refs[:total], refs[total:-3], refs[-3:]
    block = inverse.shape[1]
    slab = block // trc
    me = lax.axis_index("trc")

    def place(offset):
        return pl.ds(pl.multiple_of(slab * lax.rem(me + offset, trc), slab), slab)

    for offsets, slabs in zip(sources[:-1], kept):
        for j, offset in enumerate(offsets):
            held[:, place(offset), :] = slabs[:, j * slab : (j + 1) * slab, :]
    for _, row, values in slabs_of(1, pieces, block):
        held[row : row + values.shape[0], place(sources[-1][0]), :] = values
    turn_pieces(1, pieces, turned)
    for b in range(inverse.shape[0]):
        inverse[b] = held[b].T


def turn_last(trc, sources, pieces, kept):
    block, dtype = pieces[0].shape[2], pieces[0].dtype
    shape = (kept[0].shape[0], block, block)
    return pl.pallas_call(
        functools.partial(turn_last_kernel, trc, sources, len(pieces)),
        out_shape=(pltpu.VMEM(shape, dtype), pltpu.VMEM(shape, dtype)),
        in_specs=[VMEM] * (len(pieces) + len(kept)),
        out_specs=(VMEM, VMEM),
        scratch_shapes=[pltpu.VMEM(shape, dtype)],
        compiler_params=pltpu.CompilerParams(vmem_limit_bytes=16 * MIB),
    )(*pieces, *kept)


def after_kernel(*refs):
    del refs


def after(value, *others):
    return pl.pallas_call(
        after_kernel,
        out_shape=jax.ShapeDtypeStruct(value.shape, value.dtype),
        in_specs=[ANY] * (1 + len(others)),
        out_specs=ANY,
        input_output_aliases={0: 0},
    )(value, *others)


def ring(chunks, side):
    trc = lax.axis_size("trc")
    up = [(i, (i + 1) % trc) for i in range(trc)]
    down = [(j, i) for i, j in up]
    chunks = list(chunks)
    ahead, behind = [], []
    for i in range(len(chunks)):
        if i:
            chunks[i] = after(chunks[i], ahead[-1], behind[-1])
        ahead.append(lax.ppermute(chunks[i], "trc", up))
        behind.append(lax.ppermute(chunks[i], "trc", down))
    part, slabs, token = turn(1, chunks)
    parts, kept, sources = [part], [slabs], [(0,)]
    for distance in range(1, trc // 2):
        if distance > 1:
            both = [(lax.ppermute(p, "trc", up), lax.ppermute(q, "trc", down)) for p, q in zip(ahead, behind)]
            ahead, behind = map(list, zip(*both))
        behind[-1] = after(behind[-1], token, *side(distance, ahead))
        part, slabs, token = turn(2, [p for both in zip(ahead, behind) for p in both])
        parts.append(part)
        kept.append(slabs)
        sources.append((trc - distance, distance))
    middle = len(chunks) // 2
    last = [lax.ppermute(p, "trc", up) for p in ahead[:middle]] + [lax.ppermute(p, "trc", down) for p in behind[middle:]]
    sources.append((trc // 2,))
    part, inverse = turn_last(trc, sources, last, kept)
    parts.insert(1, part)
    return parts, inverse


def slot_offsets(trc):
    return [0, trc // 2] + [o for d in range(1, trc // 2) for o in (trc - d, d)]


def scalars_kernel(places, out, token):
    for b in range(places.shape[0]):
        for s in range(places.shape[1]):
            out[b, s] = places[b, s]
    token[...] = jnp.zeros(token.shape, token.dtype)


def scalars(places):
    return pl.pallas_call(
        scalars_kernel,
        out_shape=(pltpu.SMEM(places.shape, places.dtype), TOKEN),
        in_specs=[SMEM],
        out_specs=(SMEM, VMEM),
    )(places)


def step_kernel(mode, has_source, parts, group, *refs):
    refs = list(refs)
    places, own, before, after, field, rate = refs[:6]
    del refs[:6]
    source = refs.pop(0) if has_source else None
    matrix = [refs.pop(0) for _ in range(parts)]
    inverse = refs.pop(0)
    extra = {"plain": 0, "start": 1, "dots": 2}[mode]
    held, refs = refs[:extra], refs[extra:]
    ext = refs.pop()
    rows, slots = places.shape
    block = field.shape[1]
    tracers = field.shape[0] // rows
    pair = 2 * tracers
    size = field.shape[0]
    for i, part in enumerate((before, own, after)):
        ext[LEAD + i * size : LEAD + (i + 1) * size, :] = part[...].astype(jnp.float32)
    ext[LEAD + 3 * size : LEAD + 3 * size + pair, :] = jnp.zeros((pair, block), jnp.float32)
    upper = lax.broadcasted_iota(jnp.int32, (pair, block), 0) < tracers
    sums = [jnp.zeros((pair, block), jnp.float32) for _ in range(5)]
    for first in range(0, rows, group):
        mixed = []
        for b in range(first, first + group, 2):
            chosen = []
            for s in range(slots):
                high = ext[pl.ds(places[b, s], pair), :]
                low = ext[pl.ds(places[b + 1, s] - tracers, pair), :]
                chosen.append(jnp.where(upper, high, low).astype(jnp.bfloat16))
            picked = jnp.concatenate(chosen, axis=1)
            weights = jnp.concatenate([jnp.concatenate([part[i] for part in matrix], axis=0) for i in (b, b + 1)], axis=1)
            both = lax.dot_general(picked, weights, NN, preferred_element_type=jnp.float32)
            moved = jnp.where(upper, both[:, :block], both[:, block:])
            here = slice(b * tracers, b * tracers + pair)
            value = moved - rate[here, :] * field[here, :]
            if has_source:
                value = value + source[here, :]
            mixed.append(value.astype(jnp.bfloat16))
        for b, value in zip(range(first, first + group, 2), mixed):
            weights = jnp.concatenate([inverse[b], inverse[b + 1]], axis=1)
            both = lax.dot_general(value, weights, NN, preferred_element_type=jnp.float32)
            new = jnp.where(upper, both[:, :block], both[:, block:])
            here = slice(b * tracers, b * tracers + pair)
            if mode == "dots":
                base, image = held[0][here, :], held[1][here, :]
                one, two = image - base, new - image
                terms = (one * one, one * two, two * two, base * one, base * two)
                sums = [total + term for total, term in zip(sums, terms)]
            else:
                if mode == "start":
                    new = held[0][here, :] - new
                refs[0][here, :] = new
                refs[1][here, :] = new.astype(jnp.bfloat16)
    if mode == "dots":
        lane = lax.broadcasted_iota(jnp.int32, (1, block), 1)
        row = jnp.zeros((1, block), jnp.float32)
        for i, total in enumerate(sums):
            row = jnp.where(lane == i, jnp.sum(total, keepdims=True), row)
        refs[0][...] = jnp.broadcast_to(row[None], refs[0].shape)


def step(mode, peers, places, own, before, after, field, rate, source, matrix, *held):
    size, block = field.shape
    args = [places, own, before, after, field, rate] + ([] if source is None else [source]) + [*matrix, *held]
    if mode == "dots":
        out_shape = jax.ShapeDtypeStruct((peers, 1, block), jnp.float32)
    else:
        out_shape = tuple(jax.ShapeDtypeStruct(field.shape, t) for t in (jnp.float32, jnp.bfloat16))
    return pl.pallas_call(
        functools.partial(step_kernel, mode, source is not None, len(matrix) - 1, places.shape[0]),
        out_shape=out_shape,
        in_specs=[SMEM] + [VMEM] * (len(args) - 1),
        out_specs=VMEM if mode == "dots" else (VMEM, VMEM),
        scratch_shapes=[pltpu.VMEM((LEAD + 3 * size + 8, block), jnp.float32)],
        compiler_params=pltpu.CompilerParams(vmem_limit_bytes=24 * MIB),
    )(*args)


def finish_kernel(dots, state, base, image, out):
    row = dots[...]

    def entry(i):
        return row[:, i : i + 1]

    gram_aa, gram_ab, gram_bb, right_one, right_two = (entry(i) for i in range(5))
    determinant = gram_aa * gram_bb - gram_ab * gram_ab
    weight_one = (gram_bb * right_one - gram_ab * right_two) / determinant
    weight_two = (gram_aa * right_two - gram_ab * right_one) / determinant
    out[...] = state[...] + weight_one * base[...] + weight_two * image[...]


def body(state_guess, forcing, rate, explicit, implicit, col_index, counts):
    rows, tracers, block = state_guess.shape
    wet, trc = lax.axis_size("wet"), lax.axis_size("trc")
    start_row = lax.axis_index("wet") * rows
    positions = jnp.mod(col_index - start_row + rows + wet * rows, wet * rows)
    live = lax.broadcasted_iota(jnp.int32, col_index.shape, 1) < counts[:, None]
    places = LEAD + tracers * jnp.where(live, positions, 3 * rows)
    order = walk_order(wet)
    there = [(i, place) for i, place in enumerate(order)]
    back = [(place, i) for i, place in there]
    up = [(order[i], order[(i + 1) % wet]) for i in range(wet)]
    down = [(j, i) for i, j in up]
    flat = (rows * tracers, block)
    size = rows * tracers
    home = jnp.reshape(state_guess, flat)

    slot_order = jnp.mod(lax.axis_index("trc") + jnp.array(slot_offsets(trc), jnp.int32), trc)
    named = lax.broadcasted_iota(jnp.int32, (rows, trc, trc), 2) == slot_order[None, :, None]
    places = jnp.sum(jnp.where(named, places[:, None, :], 0), axis=2).astype(jnp.float32)
    places = jnp.pad(places, ((0, 0), (0, block - trc)))
    fields = jnp.concatenate([home] + [jnp.reshape(a, flat) for a in (forcing, rate)] + [places], axis=0)
    moved = {}

    def side(distance, arrived):
        if distance == 1:
            moved["fields"] = lax.ppermute(after(fields, arrived[0]), "wet", there)
        if distance == 2:
            state, source, rates, places = jnp.split(after(moved["fields"], arrived[1]), (size, 2 * size, 3 * size))
            rounded = state.astype(jnp.bfloat16)
            moved["start"] = (state, rounded, lax.ppermute(rounded, "wet", up), lax.ppermute(rounded, "wet", down))
            moved["rest"] = (source, rates)
            moved["places"], token = scalars(places[:, :trc].astype(jnp.int32))
            return [token]
        return []

    starts = [rows * sum(EIGHTHS[:i]) // 8 for i in range(len(EIGHTHS) + 1)]
    chunks = [jnp.concatenate([explicit[i:j, 0], implicit[i:j]], axis=1) for i, j in zip(starts, starts[1:])]
    parts, inverse = ring([lax.ppermute(p, "wet", there) for p in chunks], side)
    matrix = (*parts, inverse)
    state = moved["start"][0]
    source, rates = moved["rest"]
    places = moved["places"]

    def halo(rounded):
        return rounded, lax.ppermute(rounded, "wet", up), lax.ppermute(rounded, "wet", down)

    def run(mode, field, known, source, *held):
        for substep in range(STEPS):
            last = substep == STEPS - 1
            new = step(mode if last else "plain", wet * trc, places, *known, field, rates, source, matrix, *(held if last else ()))
            if not (last and mode == "dots"):
                field, known = new[0], halo(new[1])
                new = (field, known)
        return new

    base, known = run("start", state, moved["start"][1:], source, state)
    image, known = run("plain", base, known, None)
    dots = run("dots", image, known, None, base, image)
    base, image = (lax.ppermute(a, "wet", back) for a in (base, image))
    dots = jnp.sum(lax.all_to_all(dots, ("wet", "trc"), 0, 0), axis=0)
    out = pl.pallas_call(
        finish_kernel,
        out_shape=jax.ShapeDtypeStruct(flat, jnp.float32),
        in_specs=[VMEM] * 4,
        out_specs=VMEM,
    )(dots, home, base, image)
    return jnp.reshape(out, state_guess.shape)


def solution(mesh):
    return jax.shard_map(
        body,
        mesh=mesh,
        in_specs=(
            P("wet", "trc", None),
            P("wet", "trc", None),
            P("wet", "trc", None),
            P("wet", "trc", None, None),
            P("wet", "trc", None),
            P("wet", None),
            P("wet"),
        ),
        out_specs=P("wet", "trc", None),
        check_vma=False,
    )
```

```python
import functools
import jax
import jax.numpy as jnp
from jax import lax
from jax.experimental import pallas as pl
from jax.experimental.pallas import tpu as pltpu
from jax.sharding import PartitionSpec as P

STEPS = 4
LEAD = 8
SCALES = (2.0**-10, 2.0**-20, 2.0**-30)
MIB = 1024 * 1024
NN = (((1,), (0,)), ((), ()))
VMEM = pl.BlockSpec(memory_space=pltpu.VMEM)
SMEM = pl.BlockSpec(memory_space=pltpu.SMEM)
ANY = pl.BlockSpec(memory_space=pl.ANY)
EIGHTHS = (4, 4)
TOKEN = jax.ShapeDtypeStruct((8, 128), jnp.float32)
WALK = ((0, 3), (0, 2), (0, 1), (0, 0), (1, 0), (1, 1), (2, 1), (2, 0), (3, 0), (3, 1), (3, 2), (3, 3), (2, 3), (2, 2), (1, 2), (1, 3))


def walk_order(wet):
    if wet != 32:
        return list(range(wet))
    return [(4 * x + y) * 2 + core for x, y in WALK for core in range(2)]


def turn_pieces(count, pieces, turned):
    block = turned.shape[2]
    row = 0
    for first in range(0, len(pieces), count):
        for j in range(count):
            piece = pieces[first + j]
            for i in range(piece.shape[0]):
                turned[row + i, j * block : (j + 1) * block, :] = piece[i, :block, :].T
        row += piece.shape[0]


def slabs_of(count, pieces, block):
    for j in range(count):
        row = 0
        for piece in pieces[j::count]:
            yield j, row, piece[:, block:, :]
            row += piece.shape[0]


def turn_kernel(count, *refs):
    pieces, (turned, kept, token) = refs[:-3], refs[-3:]
    turn_pieces(count, pieces, turned)
    slab = kept.shape[1] // count
    for j, row, values in slabs_of(count, pieces, turned.shape[2]):
        kept[row : row + values.shape[0], j * slab : (j + 1) * slab, :] = values
    token[...] = jnp.zeros(token.shape, token.dtype)


def turn(count, pieces):
    height, block = pieces[0].shape[1:]
    dtype = pieces[0].dtype
    rows = sum(p.shape[0] for p in pieces) // count
    return pl.pallas_call(
        functools.partial(turn_kernel, count),
        out_shape=(pltpu.VMEM((rows, count * block, block), dtype), pltpu.VMEM((rows, count * (height - block), block), dtype), TOKEN),
        in_specs=[VMEM] * len(pieces),
        out_specs=(VMEM, VMEM, VMEM),
        compiler_params=pltpu.CompilerParams(vmem_limit_bytes=16 * MIB),
    )(*pieces)


def turn_last_kernel(trc, sources, total, *refs):
    pieces, kept, (turned, inverse, held) = refs[:total], refs[total:-3], refs[-3:]
    block = inverse.shape[1]
    slab = block // trc
    me = lax.axis_index("trc")

    def place(offset):
        return pl.ds(pl.multiple_of(slab * lax.rem(me + offset, trc), slab), slab)

    for offsets, slabs in zip(sources[:-1], kept):
        for j, offset in enumerate(offsets):
            held[:, place(offset), :] = slabs[:, j * slab : (j + 1) * slab, :]
    for _, row, values in slabs_of(1, pieces, block):
        held[row : row + values.shape[0], place(sources[-1][0]), :] = values
    turn_pieces(1, pieces, turned)
    for b in range(inverse.shape[0]):
        inverse[b] = held[b].T


def turn_last(trc, sources, pieces, kept):
    block, dtype = pieces[0].shape[2], pieces[0].dtype
    shape = (kept[0].shape[0], block, block)
    return pl.pallas_call(
        functools.partial(turn_last_kernel, trc, sources, len(pieces)),
        out_shape=(pltpu.VMEM(shape, dtype), pltpu.VMEM(shape, dtype)),
        in_specs=[VMEM] * (len(pieces) + len(kept)),
        out_specs=(VMEM, VMEM),
        scratch_shapes=[pltpu.VMEM(shape, dtype)],
        compiler_params=pltpu.CompilerParams(vmem_limit_bytes=16 * MIB),
    )(*pieces, *kept)


def after_kernel(*refs):
    del refs


def after(value, *others):
    return pl.pallas_call(
        after_kernel,
        out_shape=jax.ShapeDtypeStruct(value.shape, value.dtype),
        in_specs=[ANY] * (1 + len(others)),
        out_specs=ANY,
        input_output_aliases={0: 0},
    )(value, *others)


def ring(chunks, side):
    trc = lax.axis_size("trc")
    up = [(i, (i + 1) % trc) for i in range(trc)]
    down = [(j, i) for i, j in up]
    chunks = list(chunks)
    ahead, behind = [], []
    for i in range(len(chunks)):
        ahead.append(lax.ppermute(chunks[i], "trc", up))
        behind.append(lax.ppermute(chunks[i], "trc", down))
    part, slabs, token = turn(1, chunks)
    parts, kept, sources = [part], [slabs], [(0,)]
    for distance in range(1, trc // 2):
        if distance > 1:
            both = [(lax.ppermute(p, "trc", up), lax.ppermute(q, "trc", down)) for p, q in zip(ahead, behind)]
            ahead, behind = map(list, zip(*both))
        behind[-1] = after(behind[-1], token, *side(distance, ahead))
        part, slabs, token = turn(2, [p for both in zip(ahead, behind) for p in both])
        parts.append(part)
        kept.append(slabs)
        sources.append((trc - distance, distance))
    middle = len(chunks) // 2
    last = [lax.ppermute(p, "trc", up) for p in ahead[:middle]] + [lax.ppermute(p, "trc", down) for p in behind[middle:]]
    sources.append((trc // 2,))
    part, inverse = turn_last(trc, sources, last, kept)
    parts.insert(1, part)
    return parts, inverse


def slot_offsets(trc):
    return [0, trc // 2] + [o for d in range(1, trc // 2) for o in (trc - d, d)]


def scalars_kernel(places, out, token):
    for b in range(places.shape[0]):
        for s in range(places.shape[1]):
            out[b, s] = places[b, s]
    token[...] = jnp.zeros(token.shape, token.dtype)


def scalars(places):
    return pl.pallas_call(
        scalars_kernel,
        out_shape=(pltpu.SMEM(places.shape, places.dtype), TOKEN),
        in_specs=[SMEM],
        out_specs=(SMEM, VMEM),
    )(places)


def step_kernel(mode, has_source, parts, group, *refs):
    refs = list(refs)
    places, own, before, after, field, rate = refs[:6]
    del refs[:6]
    source = refs.pop(0) if has_source else None
    matrix = [refs.pop(0) for _ in range(parts)]
    inverse = refs.pop(0)
    extra = {"plain": 0, "start": 1, "dots": 2}[mode]
    held, refs = refs[:extra], refs[extra:]
    ext = refs.pop()
    rows, slots = places.shape
    block = field.shape[1]
    tracers = field.shape[0] // rows
    pair = 2 * tracers
    size = field.shape[0]
    for i, part in enumerate((before, own, after)):
        ext[LEAD + i * size : LEAD + (i + 1) * size, :] = part[...].astype(jnp.float32)
    ext[LEAD + 3 * size : LEAD + 3 * size + pair, :] = jnp.zeros((pair, block), jnp.float32)
    upper = lax.broadcasted_iota(jnp.int32, (pair, block), 0) < tracers
    sums = [jnp.zeros((pair, block), jnp.float32) for _ in range(5)]
    for first in range(0, rows, group):
        mixed = []
        for b in range(first, first + group, 2):
            chosen = []
            for s in range(slots):
                high = ext[pl.ds(places[b, s], pair), :]
                low = ext[pl.ds(places[b + 1, s] - tracers, pair), :]
                chosen.append(jnp.where(upper, high, low).astype(jnp.bfloat16))
            picked = jnp.concatenate(chosen, axis=1)
            weights = jnp.concatenate([jnp.concatenate([part[i] for part in matrix], axis=0) for i in (b, b + 1)], axis=1)
            both = lax.dot_general(picked, weights, NN, preferred_element_type=jnp.float32)
            moved = jnp.where(upper, both[:, :block], both[:, block:])
            here = slice(b * tracers, b * tracers + pair)
            value = moved - rate[here, :] * field[here, :]
            if has_source:
                value = value + source[here, :]
            mixed.append(value.astype(jnp.bfloat16))
        for b, value in zip(range(first, first + group, 2), mixed):
            weights = jnp.concatenate([inverse[b], inverse[b + 1]], axis=1)
            both = lax.dot_general(value, weights, NN, preferred_element_type=jnp.float32)
            new = jnp.where(upper, both[:, :block], both[:, block:])
            here = slice(b * tracers, b * tracers + pair)
            if mode == "dots":
                base, image = held[0][here, :], held[1][here, :]
                one, two = (image - base) * SCALES[1], (new - image) * SCALES[2]
                base = base * SCALES[0]
                terms = (one * one, one * two, two * two, base * one, base * two)
                sums = [total + term for total, term in zip(sums, terms)]
            else:
                if mode == "start":
                    new = held[0][here, :] - new
                refs[0][here, :] = new
                refs[1][here, :] = new.astype(jnp.bfloat16)
    if mode == "dots":
        lane = lax.broadcasted_iota(jnp.int32, (1, block), 1)
        row = jnp.zeros((1, block), jnp.float32)
        for i, total in enumerate(sums):
            row = jnp.where(lane == i, jnp.sum(total, keepdims=True), row)
        refs[0][...] = jnp.broadcast_to(row[None], refs[0].shape)


def step(mode, peers, places, own, before, after, field, rate, source, matrix, *held):
    size, block = field.shape
    args = [places, own, before, after, field, rate] + ([] if source is None else [source]) + [*matrix, *held]
    if mode == "dots":
        out_shape = jax.ShapeDtypeStruct((peers, 1, block), jnp.float32)
    else:
        out_shape = tuple(jax.ShapeDtypeStruct(field.shape, t) for t in (jnp.float32, jnp.bfloat16))
    return pl.pallas_call(
        functools.partial(step_kernel, mode, source is not None, len(matrix) - 1, places.shape[0]),
        out_shape=out_shape,
        in_specs=[SMEM] + [VMEM] * (len(args) - 1),
        out_specs=VMEM if mode == "dots" else (VMEM, VMEM),
        scratch_shapes=[pltpu.VMEM((LEAD + 3 * size + 8, block), jnp.float32)],
        compiler_params=pltpu.CompilerParams(vmem_limit_bytes=24 * MIB),
    )(*args)


def finish_kernel(dots, state, base, image, out):
    row = jnp.sum(dots[...], axis=0)
    gram_aa, gram_ab, gram_bb, right_one, right_two = (row[:, i : i + 1] for i in range(5))
    unit_one, unit_two = 1.0 / jnp.sqrt(gram_aa), 1.0 / jnp.sqrt(gram_bb)
    cosine = gram_ab * unit_one * unit_two
    right_one, right_two = right_one * unit_one, right_two * unit_two
    determinant = (1.0 - cosine) * (1.0 + cosine)
    weight_one = (right_one - cosine * right_two) / determinant * (unit_one * (SCALES[1] / SCALES[0]))
    weight_two = (right_two - cosine * right_one) / determinant * (unit_two * (SCALES[2] / SCALES[0]))
    out[...] = state[...] + weight_one * base[...] + weight_two * image[...]


def body(state_guess, forcing, rate, explicit, implicit, col_index, counts):
    rows, tracers, block = state_guess.shape
    wet, trc = lax.axis_size("wet"), lax.axis_size("trc")
    start_row = lax.axis_index("wet") * rows
    positions = jnp.mod(col_index - start_row + rows + wet * rows, wet * rows)
    live = lax.broadcasted_iota(jnp.int32, col_index.shape, 1) < counts[:, None]
    places = LEAD + tracers * jnp.where(live, positions, 3 * rows)
    order = walk_order(wet)
    there = [(i, place) for i, place in enumerate(order)]
    back = [(place, i) for i, place in there]
    up = [(order[i], order[(i + 1) % wet]) for i in range(wet)]
    down = [(j, i) for i, j in up]
    flat = (rows * tracers, block)
    size = rows * tracers
    home = jnp.reshape(state_guess, flat)

    slot_order = jnp.mod(lax.axis_index("trc") + jnp.array(slot_offsets(trc), jnp.int32), trc)
    named = lax.broadcasted_iota(jnp.int32, (rows, trc, trc), 2) == slot_order[None, :, None]
    places = jnp.sum(jnp.where(named, places[:, None, :], 0), axis=2).astype(jnp.float32)
    places = jnp.pad(places, ((0, 0), (0, block - trc)))
    fields = jnp.concatenate([home] + [jnp.reshape(a, flat) for a in (forcing, rate)] + [places], axis=0)
    moved = {}

    def side(distance, arrived):
        if distance == 1:
            moved["fields"] = lax.ppermute(after(fields, arrived[0]), "wet", there)
        if distance == 2:
            state, source, rates, places = jnp.split(after(moved["fields"], arrived[1]), (size, 2 * size, 3 * size))
            rounded = state.astype(jnp.bfloat16)
            moved["start"] = (state, rounded, lax.ppermute(rounded, "wet", up), lax.ppermute(rounded, "wet", down))
            moved["rest"] = (source, rates)
            moved["places"], token = scalars(places[:, :trc].astype(jnp.int32))
            return [token]
        return []

    starts = [rows * sum(EIGHTHS[:i]) // 8 for i in range(len(EIGHTHS) + 1)]
    chunks = [jnp.concatenate([explicit[i:j, 0], implicit[i:j]], axis=1) for i, j in zip(starts, starts[1:])]
    parts, inverse = ring([lax.ppermute(p, "wet", there) for p in chunks], side)
    matrix = (*parts, inverse)
    state = moved["start"][0]
    source, rates = moved["rest"]
    places = moved["places"]

    def halo(rounded):
        return rounded, lax.ppermute(rounded, "wet", up), lax.ppermute(rounded, "wet", down)

    def run(mode, field, known, source, *held):
        for substep in range(STEPS):
            last = substep == STEPS - 1
            new = step(mode if last else "plain", wet * trc, places, *known, field, rates, source, matrix, *(held if last else ()))
            if not (last and mode == "dots"):
                field, known = new[0], halo(new[1])
                new = (field, known)
        return new

    base, known = run("start", state, moved["start"][1:], source, state)
    image, known = run("plain", base, known, None)
    dots = run("dots", image, known, None, base, image)
    base, image = (lax.ppermute(a, "wet", back) for a in (base, image))
    dots = lax.all_to_all(dots, ("wet", "trc"), 0, 0)
    out = pl.pallas_call(
        finish_kernel,
        out_shape=jax.ShapeDtypeStruct(flat, jnp.float32),
        in_specs=[VMEM] * 4,
        out_specs=VMEM,
    )(dots, home, base, image)
    return jnp.reshape(out, state_guess.shape)


def solution(mesh):
    return jax.shard_map(
        body,
        mesh=mesh,
        in_specs=(
            P("wet", "trc", None),
            P("wet", "trc", None),
            P("wet", "trc", None),
            P("wet", "trc", None, None),
            P("wet", "trc", None),
            P("wet", None),
            P("wet"),
        ),
        out_specs=P("wet", "trc", None),
        check_vma=False,
    )
```

```python
import functools
import jax
import jax.numpy as jnp
from jax import lax
from jax.experimental import pallas as pl
from jax.experimental.pallas import tpu as pltpu
from jax.sharding import PartitionSpec as P

STEPS = 4
LEAD = 8
SCALES = (2.0**-10, 2.0**-20, 2.0**-30)
MIB = 1024 * 1024
NN = (((1,), (0,)), ((), ()))
VMEM = pl.BlockSpec(memory_space=pltpu.VMEM)
SMEM = pl.BlockSpec(memory_space=pltpu.SMEM)
ANY = pl.BlockSpec(memory_space=pl.ANY)
EIGHTHS = (4, 4)
TOKEN = jax.ShapeDtypeStruct((8, 128), jnp.float32)
WALK = ((0, 3), (0, 2), (0, 1), (0, 0), (1, 0), (1, 1), (2, 1), (2, 0), (3, 0), (3, 1), (3, 2), (3, 3), (2, 3), (2, 2), (1, 2), (1, 3))


def walk_order(wet):
    if wet != 32:
        return list(range(wet))
    return [(4 * x + y) * 2 + core for x, y in WALK for core in range(2)]


def turn_pieces(count, pieces, turned):
    block = turned.shape[2]
    row = 0
    for first in range(0, len(pieces), count):
        for j in range(count):
            piece = pieces[first + j]
            for i in range(piece.shape[0]):
                turned[row + i, j * block : (j + 1) * block, :] = piece[i, :block, :].T
        row += piece.shape[0]


def slabs_of(count, pieces, block):
    for j in range(count):
        row = 0
        for piece in pieces[j::count]:
            yield j, row, piece[:, block:, :]
            row += piece.shape[0]


def turn_kernel(count, *refs):
    pieces, (turned, kept, token) = refs[:-3], refs[-3:]
    turn_pieces(count, pieces, turned)
    slab = kept.shape[1] // count
    for j, row, values in slabs_of(count, pieces, turned.shape[2]):
        kept[row : row + values.shape[0], j * slab : (j + 1) * slab, :] = values
    token[...] = jnp.zeros(token.shape, token.dtype)


def turn(count, pieces):
    height, block = pieces[0].shape[1:]
    dtype = pieces[0].dtype
    rows = sum(p.shape[0] for p in pieces) // count
    return pl.pallas_call(
        functools.partial(turn_kernel, count),
        out_shape=(pltpu.VMEM((rows, count * block, block), dtype), pltpu.VMEM((rows, count * (height - block), block), dtype), TOKEN),
        in_specs=[VMEM] * len(pieces),
        out_specs=(VMEM, VMEM, VMEM),
        compiler_params=pltpu.CompilerParams(vmem_limit_bytes=16 * MIB),
    )(*pieces)


def turn_last_kernel(trc, sources, total, *refs):
    pieces, kept, (turned, inverse, held) = refs[:total], refs[total:-3], refs[-3:]
    block = inverse.shape[1]
    slab = block // trc
    me = lax.axis_index("trc")

    def place(offset):
        return pl.ds(pl.multiple_of(slab * lax.rem(me + offset, trc), slab), slab)

    for offsets, slabs in zip(sources[:-1], kept):
        for j, offset in enumerate(offsets):
            held[:, place(offset), :] = slabs[:, j * slab : (j + 1) * slab, :]
    for _, row, values in slabs_of(1, pieces, block):
        held[row : row + values.shape[0], place(sources[-1][0]), :] = values
    turn_pieces(1, pieces, turned)
    for b in range(inverse.shape[0]):
        inverse[b] = held[b].T


def turn_last(trc, sources, pieces, kept):
    block, dtype = pieces[0].shape[2], pieces[0].dtype
    shape = (kept[0].shape[0], block, block)
    return pl.pallas_call(
        functools.partial(turn_last_kernel, trc, sources, len(pieces)),
        out_shape=(pltpu.VMEM(shape, dtype), pltpu.VMEM(shape, dtype)),
        in_specs=[VMEM] * (len(pieces) + len(kept)),
        out_specs=(VMEM, VMEM),
        scratch_shapes=[pltpu.VMEM(shape, dtype)],
        compiler_params=pltpu.CompilerParams(vmem_limit_bytes=16 * MIB),
    )(*pieces, *kept)


def after_kernel(*refs):
    del refs


def after(value, *others):
    return pl.pallas_call(
        after_kernel,
        out_shape=jax.ShapeDtypeStruct(value.shape, value.dtype),
        in_specs=[ANY] * (1 + len(others)),
        out_specs=ANY,
        input_output_aliases={0: 0},
    )(value, *others)


def ring(chunks, side):
    trc = lax.axis_size("trc")
    up = [(i, (i + 1) % trc) for i in range(trc)]
    down = [(j, i) for i, j in up]
    chunks = list(chunks)
    ahead, behind = [], []
    for i in range(len(chunks)):
        ahead.append(lax.ppermute(chunks[i], "trc", up))
        behind.append(lax.ppermute(chunks[i], "trc", down))
    part, slabs, token = turn(1, chunks)
    parts, kept, sources = [part], [slabs], [(0,)]
    for distance in range(1, trc // 2):
        if distance > 1:
            both = [(lax.ppermute(p, "trc", up), lax.ppermute(q, "trc", down)) for p, q in zip(ahead, behind)]
            ahead, behind = map(list, zip(*both))
        behind[-1] = after(behind[-1], token, *side(distance, ahead))
        part, slabs, token = turn(2, [p for both in zip(ahead, behind) for p in both])
        parts.append(part)
        kept.append(slabs)
        sources.append((trc - distance, distance))
    middle = len(chunks) // 2
    last = [lax.ppermute(p, "trc", up) for p in ahead[:middle]] + [lax.ppermute(p, "trc", down) for p in behind[middle:]]
    sources.append((trc // 2,))
    part, inverse = turn_last(trc, sources, last, kept)
    parts.insert(1, part)
    return parts, inverse


def slot_offsets(trc):
    return [0, trc // 2] + [o for d in range(1, trc // 2) for o in (trc - d, d)]


def scalars_kernel(places, out, token):
    for b in range(places.shape[0]):
        for s in range(places.shape[1]):
            out[b, s] = places[b, s]
    token[...] = jnp.zeros(token.shape, token.dtype)


def scalars(places):
    return pl.pallas_call(
        scalars_kernel,
        out_shape=(pltpu.SMEM(places.shape, places.dtype), TOKEN),
        in_specs=[SMEM],
        out_specs=(SMEM, VMEM),
    )(places)


def step_kernel(mode, has_source, parts, group, *refs):
    refs = list(refs)
    places, own, before, after, field, rate = refs[:6]
    del refs[:6]
    source = refs.pop(0) if has_source else None
    matrix = [refs.pop(0) for _ in range(parts)]
    inverse = refs.pop(0)
    extra = {"plain": 0, "start": 1, "dots": 2}[mode]
    held, refs = refs[:extra], refs[extra:]
    ext = refs.pop()
    rows, slots = places.shape
    block = field.shape[1]
    tracers = field.shape[0] // rows
    pair = 2 * tracers
    size = field.shape[0]
    for i, part in enumerate((before, own, after)):
        ext[LEAD + i * size : LEAD + (i + 1) * size, :] = part[...].astype(jnp.float32)
    ext[LEAD + 3 * size : LEAD + 3 * size + pair, :] = jnp.zeros((pair, block), jnp.float32)
    upper = lax.broadcasted_iota(jnp.int32, (pair, block), 0) < tracers
    sums = [jnp.zeros((pair, block), jnp.float32) for _ in range(5)]
    for first in range(0, rows, group):
        mixed = []
        for b in range(first, first + group, 2):
            chosen = []
            for s in range(slots):
                high = ext[pl.ds(places[b, s], pair), :]
                low = ext[pl.ds(places[b + 1, s] - tracers, pair), :]
                chosen.append(jnp.where(upper, high, low).astype(jnp.bfloat16))
            picked = jnp.concatenate(chosen, axis=1)
            weights = jnp.concatenate([jnp.concatenate([part[i] for part in matrix], axis=0) for i in (b, b + 1)], axis=1)
            both = lax.dot_general(picked, weights, NN, preferred_element_type=jnp.float32)
            moved = jnp.where(upper, both[:, :block], both[:, block:])
            here = slice(b * tracers, b * tracers + pair)
            value = moved - rate[here, :] * field[here, :]
            if has_source:
                value = value + source[here, :]
            mixed.append(value.astype(jnp.bfloat16))
        for b, value in zip(range(first, first + group, 2), mixed):
            weights = jnp.concatenate([inverse[b], inverse[b + 1]], axis=1)
            both = lax.dot_general(value, weights, NN, preferred_element_type=jnp.float32)
            new = jnp.where(upper, both[:, :block], both[:, block:])
            here = slice(b * tracers, b * tracers + pair)
            if mode == "dots":
                base, image = held[0][here, :], held[1][here, :]
                one, two = (image - base) * SCALES[1], (new - image) * SCALES[2]
                base = base * SCALES[0]
                terms = (one * one, one * two, two * two, base * one, base * two)
                sums = [total + term for total, term in zip(sums, terms)]
            else:
                if mode == "start":
                    new = held[0][here, :] - new
                refs[0][here, :] = new
                refs[1][here, :] = new.astype(jnp.bfloat16)
    if mode == "dots":
        lane = lax.broadcasted_iota(jnp.int32, (1, block), 1)
        row = jnp.zeros((1, block), jnp.float32)
        for i, total in enumerate(sums):
            row = jnp.where(lane == i, jnp.sum(total, keepdims=True), row)
        refs[0][...] = jnp.broadcast_to(row[None], refs[0].shape)


def step(mode, peers, places, own, before, after, field, rate, source, matrix, *held):
    size, block = field.shape
    args = [places, own, before, after, field, rate] + ([] if source is None else [source]) + [*matrix, *held]
    if mode == "dots":
        out_shape = jax.ShapeDtypeStruct((peers, 1, block), jnp.float32)
    else:
        out_shape = tuple(jax.ShapeDtypeStruct(field.shape, t) for t in (jnp.float32, jnp.bfloat16))
    return pl.pallas_call(
        functools.partial(step_kernel, mode, source is not None, len(matrix) - 1, places.shape[0]),
        out_shape=out_shape,
        in_specs=[SMEM] + [VMEM] * (len(args) - 1),
        out_specs=VMEM if mode == "dots" else (VMEM, VMEM),
        scratch_shapes=[pltpu.VMEM((LEAD + 3 * size + 8, block), jnp.float32)],
        compiler_params=pltpu.CompilerParams(vmem_limit_bytes=24 * MIB),
    )(*args)


def finish_kernel(dots, state, base, image, out):
    row = jnp.sum(dots[...], axis=0)
    gram_aa, gram_ab, gram_bb, right_one, right_two = (row[:, i : i + 1] for i in range(5))
    unit_one, unit_two = 1.0 / jnp.sqrt(gram_aa), 1.0 / jnp.sqrt(gram_bb)
    cosine = gram_ab * unit_one * unit_two
    right_one, right_two = right_one * unit_one, right_two * unit_two
    determinant = (1.0 - cosine) * (1.0 + cosine)
    weight_one = (right_one - cosine * right_two) / determinant * (unit_one * (SCALES[1] / SCALES[0]))
    weight_two = (right_two - cosine * right_one) / determinant * (unit_two * (SCALES[2] / SCALES[0]))
    out[...] = state[...] + weight_one * base[...] + weight_two * image[...]


def body(state_guess, forcing, rate, explicit, implicit, col_index, counts):
    rows, tracers, block = state_guess.shape
    wet, trc = lax.axis_size("wet"), lax.axis_size("trc")
    start_row = lax.axis_index("wet") * rows
    positions = jnp.mod(col_index - start_row + rows + wet * rows, wet * rows)
    live = lax.broadcasted_iota(jnp.int32, col_index.shape, 1) < counts[:, None]
    places = LEAD + tracers * jnp.where(live, positions, 3 * rows)
    order = walk_order(wet)
    there = [(i, place) for i, place in enumerate(order)]
    back = [(place, i) for i, place in there]
    up = [(order[i], order[(i + 1) % wet]) for i in range(wet)]
    down = [(j, i) for i, j in up]
    flat = (rows * tracers, block)
    size = rows * tracers
    home = jnp.reshape(state_guess, flat)

    slot_order = jnp.mod(lax.axis_index("trc") + jnp.array(slot_offsets(trc), jnp.int32), trc)
    named = lax.broadcasted_iota(jnp.int32, (rows, trc, trc), 2) == slot_order[None, :, None]
    places = jnp.sum(jnp.where(named, places[:, None, :], 0), axis=2).astype(jnp.float32)
    places = jnp.pad(places, ((0, 0), (0, block - trc)))
    fields = jnp.concatenate([home] + [jnp.reshape(a, flat) for a in (forcing, rate)] + [places], axis=0)
    fields = lax.ppermute(fields, "wet", there)
    moved = {}

    def side(distance, arrived):
        if distance == 1:
            moved["fields"] = fields
            return [fields]
        if distance == 2:
            state, source, rates, places = jnp.split(after(moved["fields"], arrived[1]), (size, 2 * size, 3 * size))
            rounded = state.astype(jnp.bfloat16)
            moved["start"] = (state, rounded, lax.ppermute(rounded, "wet", up), lax.ppermute(rounded, "wet", down))
            moved["rest"] = (source, rates)
            moved["places"], token = scalars(places[:, :trc].astype(jnp.int32))
            return [token]
        return []

    starts = [rows * sum(EIGHTHS[:i]) // 8 for i in range(len(EIGHTHS) + 1)]
    chunks = [jnp.concatenate([explicit[i:j, 0], implicit[i:j]], axis=1) for i, j in zip(starts, starts[1:])]
    parts, inverse = ring([lax.ppermute(p, "wet", there) for p in chunks], side)
    matrix = (*parts, inverse)
    state = moved["start"][0]
    source, rates = moved["rest"]
    places = moved["places"]

    def halo(rounded):
        return rounded, lax.ppermute(rounded, "wet", up), lax.ppermute(rounded, "wet", down)

    def run(mode, field, known, source, *held):
        for substep in range(STEPS):
            last = substep == STEPS - 1
            new = step(mode if last else "plain", wet * trc, places, *known, field, rates, source, matrix, *(held if last else ()))
            if not (last and mode == "dots"):
                field, known = new[0], halo(new[1])
                new = (field, known)
        return new

    base, known = run("start", state, moved["start"][1:], source, state)
    image, known = run("plain", base, known, None)
    dots = run("dots", image, known, None, base, image)
    base, image = (lax.ppermute(a, "wet", back) for a in (base, image))
    dots = lax.all_to_all(dots, ("wet", "trc"), 0, 0)
    out = pl.pallas_call(
        finish_kernel,
        out_shape=jax.ShapeDtypeStruct(flat, jnp.float32),
        in_specs=[VMEM] * 4,
        out_specs=VMEM,
    )(dots, home, base, image)
    return jnp.reshape(out, state_guess.shape)


def solution(mesh):
    return jax.shard_map(
        body,
        mesh=mesh,
        in_specs=(
            P("wet", "trc", None),
            P("wet", "trc", None),
            P("wet", "trc", None),
            P("wet", "trc", None, None),
            P("wet", "trc", None),
            P("wet", None),
            P("wet"),
        ),
        out_specs=P("wet", "trc", None),
        check_vma=False,
    )
```

```python
import functools
import jax
import jax.numpy as jnp
from jax import lax
from jax.experimental import pallas as pl
from jax.experimental.pallas import tpu as pltpu
from jax.sharding import PartitionSpec as P

STEPS = 4
LEAD = 8
SCALES = (2.0**-10, 2.0**-20, 2.0**-30)
MIB = 1024 * 1024
NN = (((1,), (0,)), ((), ()))
VMEM = pl.BlockSpec(memory_space=pltpu.VMEM)
SMEM = pl.BlockSpec(memory_space=pltpu.SMEM)
ANY = pl.BlockSpec(memory_space=pl.ANY)
EIGHTHS = (4, 4)
TOKEN = jax.ShapeDtypeStruct((8, 128), jnp.float32)
WALK = ((0, 3), (0, 2), (0, 1), (0, 0), (1, 0), (1, 1), (2, 1), (2, 0), (3, 0), (3, 1), (3, 2), (3, 3), (2, 3), (2, 2), (1, 2), (1, 3))


def walk_order(wet):
    if wet != 32:
        return list(range(wet))
    return [(4 * x + y) * 2 + core for x, y in WALK for core in range(2)]


def turn_pieces(count, pieces, turned):
    block = turned.shape[2]
    row = 0
    for first in range(0, len(pieces), count):
        for j in range(count):
            piece = pieces[first + j]
            for i in range(piece.shape[0]):
                turned[row + i, j * block : (j + 1) * block, :] = piece[i, :block, :].T
        row += piece.shape[0]


def slabs_of(count, pieces, block):
    for j in range(count):
        row = 0
        for piece in pieces[j::count]:
            yield j, row, piece[:, block:, :]
            row += piece.shape[0]


def turn_kernel(count, *refs):
    pieces, (turned, kept, token) = refs[:-3], refs[-3:]
    turn_pieces(count, pieces, turned)
    slab = kept.shape[1] // count
    for j, row, values in slabs_of(count, pieces, turned.shape[2]):
        kept[row : row + values.shape[0], j * slab : (j + 1) * slab, :] = values
    token[...] = jnp.zeros(token.shape, token.dtype)


def turn(count, pieces):
    height, block = pieces[0].shape[1:]
    dtype = pieces[0].dtype
    rows = sum(p.shape[0] for p in pieces) // count
    return pl.pallas_call(
        functools.partial(turn_kernel, count),
        out_shape=(pltpu.VMEM((rows, count * block, block), dtype), pltpu.VMEM((rows, count * (height - block), block), dtype), TOKEN),
        in_specs=[VMEM] * len(pieces),
        out_specs=(VMEM, VMEM, VMEM),
        compiler_params=pltpu.CompilerParams(vmem_limit_bytes=16 * MIB),
    )(*pieces)


def turn_last_kernel(trc, sources, total, *refs):
    pieces, kept, (turned, inverse, held) = refs[:total], refs[total:-3], refs[-3:]
    block = inverse.shape[1]
    slab = block // trc
    me = lax.axis_index("trc")

    def place(offset):
        return pl.ds(pl.multiple_of(slab * lax.rem(me + offset, trc), slab), slab)

    for offsets, slabs in zip(sources[:-1], kept):
        for j, offset in enumerate(offsets):
            held[:, place(offset), :] = slabs[:, j * slab : (j + 1) * slab, :]
    for _, row, values in slabs_of(1, pieces, block):
        held[row : row + values.shape[0], place(sources[-1][0]), :] = values
    turn_pieces(1, pieces, turned)
    for b in range(inverse.shape[0]):
        inverse[b] = held[b].T


def turn_last(trc, sources, pieces, kept):
    block, dtype = pieces[0].shape[2], pieces[0].dtype
    shape = (kept[0].shape[0], block, block)
    return pl.pallas_call(
        functools.partial(turn_last_kernel, trc, sources, len(pieces)),
        out_shape=(pltpu.VMEM(shape, dtype), pltpu.VMEM(shape, dtype)),
        in_specs=[VMEM] * (len(pieces) + len(kept)),
        out_specs=(VMEM, VMEM),
        scratch_shapes=[pltpu.VMEM(shape, dtype)],
        compiler_params=pltpu.CompilerParams(vmem_limit_bytes=16 * MIB),
    )(*pieces, *kept)


def after_kernel(*refs):
    del refs


def after(value, *others):
    return pl.pallas_call(
        after_kernel,
        out_shape=jax.ShapeDtypeStruct(value.shape, value.dtype),
        in_specs=[ANY] + [VMEM if other.shape == TOKEN.shape else ANY for other in others],
        out_specs=ANY,
        input_output_aliases={0: 0},
    )(value, *others)


def ring(chunks, side):
    trc = lax.axis_size("trc")
    up = [(i, (i + 1) % trc) for i in range(trc)]
    down = [(j, i) for i, j in up]
    chunks = list(chunks)
    ahead, behind = [], []
    for i in range(len(chunks)):
        ahead.append(lax.ppermute(chunks[i], "trc", up))
        behind.append(lax.ppermute(chunks[i], "trc", down))
    part, slabs, token = turn(1, chunks)
    parts, kept, sources = [part], [slabs], [(0,)]
    for distance in range(1, trc // 2):
        if distance > 1:
            both = [(lax.ppermute(p, "trc", up), lax.ppermute(q, "trc", down)) for p, q in zip(ahead, behind)]
            ahead, behind = map(list, zip(*both))
        behind[-1] = after(behind[-1], token, *side(distance, ahead))
        part, slabs, token = turn(2, [p for both in zip(ahead, behind) for p in both])
        parts.append(part)
        kept.append(slabs)
        sources.append((trc - distance, distance))
    middle = len(chunks) // 2
    last = [lax.ppermute(p, "trc", up) for p in ahead[:middle]] + [lax.ppermute(p, "trc", down) for p in behind[middle:]]
    sources.append((trc // 2,))
    part, inverse = turn_last(trc, sources, last, kept)
    parts.insert(1, part)
    return parts, inverse


def slot_offsets(trc):
    return [0, trc // 2] + [o for d in range(1, trc // 2) for o in (trc - d, d)]


def scalars_kernel(places, out, token):
    for b in range(places.shape[0]):
        for s in range(places.shape[1]):
            out[b, s] = places[b, s]
    token[...] = jnp.zeros(token.shape, token.dtype)


def scalars(places):
    return pl.pallas_call(
        scalars_kernel,
        out_shape=(pltpu.SMEM(places.shape, places.dtype), TOKEN),
        in_specs=[SMEM],
        out_specs=(SMEM, VMEM),
    )(places)


def step_kernel(mode, has_source, parts, group, *refs):
    refs = list(refs)
    places, own, before, after, field, rate = refs[:6]
    del refs[:6]
    source = refs.pop(0) if has_source else None
    matrix = [refs.pop(0) for _ in range(parts)]
    inverse = refs.pop(0)
    extra = {"plain": 0, "start": 1, "dots": 2}[mode]
    held, refs = refs[:extra], refs[extra:]
    ext = refs.pop()
    rows, slots = places.shape
    block = field.shape[1]
    tracers = field.shape[0] // rows
    pair = 2 * tracers
    size = field.shape[0]
    for i, part in enumerate((before, own, after)):
        ext[LEAD + i * size : LEAD + (i + 1) * size, :] = part[...].astype(jnp.float32)
    ext[LEAD + 3 * size : LEAD + 3 * size + pair, :] = jnp.zeros((pair, block), jnp.float32)
    upper = lax.broadcasted_iota(jnp.int32, (pair, block), 0) < tracers
    sums = [jnp.zeros((pair, block), jnp.float32) for _ in range(5)]
    for first in range(0, rows, group):
        mixed = []
        for b in range(first, first + group, 2):
            chosen = []
            for s in range(slots):
                high = ext[pl.ds(places[b, s], pair), :]
                low = ext[pl.ds(places[b + 1, s] - tracers, pair), :]
                chosen.append(jnp.where(upper, high, low).astype(jnp.bfloat16))
            picked = jnp.concatenate(chosen, axis=1)
            weights = jnp.concatenate([jnp.concatenate([part[i] for part in matrix], axis=0) for i in (b, b + 1)], axis=1)
            both = lax.dot_general(picked, weights, NN, preferred_element_type=jnp.float32)
            moved = jnp.where(upper, both[:, :block], both[:, block:])
            here = slice(b * tracers, b * tracers + pair)
            value = moved - rate[here, :] * field[here, :]
            if has_source:
                value = value + source[here, :]
            mixed.append(value.astype(jnp.bfloat16))
        for b, value in zip(range(first, first + group, 2), mixed):
            weights = jnp.concatenate([inverse[b], inverse[b + 1]], axis=1)
            both = lax.dot_general(value, weights, NN, preferred_element_type=jnp.float32)
            new = jnp.where(upper, both[:, :block], both[:, block:])
            here = slice(b * tracers, b * tracers + pair)
            if mode == "dots":
                base, image = held[0][here, :], held[1][here, :]
                one, two = (image - base) * SCALES[1], (new - image) * SCALES[2]
                base = base * SCALES[0]
                terms = (one * one, one * two, two * two, base * one, base * two)
                sums = [total + term for total, term in zip(sums, terms)]
            else:
                if mode == "start":
                    new = held[0][here, :] - new
                refs[0][here, :] = new
                refs[1][here, :] = new.astype(jnp.bfloat16)
    if mode == "dots":
        lane = lax.broadcasted_iota(jnp.int32, (1, block), 1)
        row = jnp.zeros((1, block), jnp.float32)
        for i, total in enumerate(sums):
            row = jnp.where(lane == i, jnp.sum(total, keepdims=True), row)
        refs[0][...] = row


def step(mode, places, own, before, after, field, rate, source, matrix, *held):
    size, block = field.shape
    args = [places, own, before, after, field, rate] + ([] if source is None else [source]) + [*matrix, *held]
    if mode == "dots":
        out_shape = jax.ShapeDtypeStruct((1, block), jnp.float32)
    else:
        out_shape = tuple(jax.ShapeDtypeStruct(field.shape, t) for t in (jnp.float32, jnp.bfloat16))
    return pl.pallas_call(
        functools.partial(step_kernel, mode, source is not None, len(matrix) - 1, places.shape[0]),
        out_shape=out_shape,
        in_specs=[SMEM] + [VMEM] * (len(args) - 1),
        out_specs=VMEM if mode == "dots" else (VMEM, VMEM),
        scratch_shapes=[pltpu.VMEM((LEAD + 3 * size + 8, block), jnp.float32)],
        compiler_params=pltpu.CompilerParams(vmem_limit_bytes=24 * MIB),
    )(*args)


def finish_kernel(dots, state, base, image, out):
    row = jnp.sum(dots[...], axis=0)
    gram_aa, gram_ab, gram_bb, right_one, right_two = (row[:, i : i + 1] for i in range(5))
    unit_one, unit_two = 1.0 / jnp.sqrt(gram_aa), 1.0 / jnp.sqrt(gram_bb)
    cosine = gram_ab * unit_one * unit_two
    right_one, right_two = right_one * unit_one, right_two * unit_two
    determinant = (1.0 - cosine) * (1.0 + cosine)
    weight_one = (right_one - cosine * right_two) / determinant * (unit_one * (SCALES[1] / SCALES[0]))
    weight_two = (right_two - cosine * right_one) / determinant * (unit_two * (SCALES[2] / SCALES[0]))
    out[...] = state[...] + weight_one * base[...] + weight_two * image[...]


def body(state_guess, forcing, rate, explicit, implicit, col_index, counts):
    rows, tracers, block = state_guess.shape
    wet, trc = lax.axis_size("wet"), lax.axis_size("trc")
    start_row = lax.axis_index("wet") * rows
    positions = jnp.mod(col_index - start_row + rows + wet * rows, wet * rows)
    live = lax.broadcasted_iota(jnp.int32, col_index.shape, 1) < counts[:, None]
    places = LEAD + tracers * jnp.where(live, positions, 3 * rows)
    order = walk_order(wet)
    there = [(i, place) for i, place in enumerate(order)]
    back = [(place, i) for i, place in there]
    up = [(order[i], order[(i + 1) % wet]) for i in range(wet)]
    down = [(j, i) for i, j in up]
    flat = (rows * tracers, block)
    size = rows * tracers
    home = jnp.reshape(state_guess, flat)

    slot_order = jnp.mod(lax.axis_index("trc") + jnp.array(slot_offsets(trc), jnp.int32), trc)
    named = lax.broadcasted_iota(jnp.int32, (rows, trc, trc), 2) == slot_order[None, :, None]
    places = jnp.sum(jnp.where(named, places[:, None, :], 0), axis=2).astype(jnp.float32)
    places = jnp.pad(places, ((0, 0), (0, block - trc)))
    fields = jnp.concatenate([home] + [jnp.reshape(a, flat) for a in (forcing, rate)] + [places], axis=0)
    fields = lax.ppermute(fields, "wet", there)
    moved = {}

    def side(distance, arrived):
        if distance == 1:
            moved["fields"] = fields
            return [fields]
        if distance == 2:
            state, source, rates, places = jnp.split(after(moved["fields"], arrived[1]), (size, 2 * size, 3 * size))
            rounded = state.astype(jnp.bfloat16)
            moved["start"] = (state, rounded, lax.ppermute(rounded, "wet", up), lax.ppermute(rounded, "wet", down))
            moved["rest"] = (source, rates)
            moved["places"], token = scalars(places[:, :trc].astype(jnp.int32))
            return [token]
        return []

    starts = [rows * sum(EIGHTHS[:i]) // 8 for i in range(len(EIGHTHS) + 1)]
    chunks = [jnp.concatenate([explicit[i:j, 0], implicit[i:j]], axis=1) for i, j in zip(starts, starts[1:])]
    parts, inverse = ring([lax.ppermute(p, "wet", there) for p in chunks], side)
    matrix = (*parts, inverse)
    state = moved["start"][0]
    source, rates = moved["rest"]
    places = moved["places"]

    def halo(rounded):
        return rounded, lax.ppermute(rounded, "wet", up), lax.ppermute(rounded, "wet", down)

    def run(mode, field, known, source, *held):
        for substep in range(STEPS):
            last = substep == STEPS - 1
            new = step(mode if last else "plain", places, *known, field, rates, source, matrix, *(held if last else ()))
            if not (last and mode == "dots"):
                field, known = new[0], halo(new[1])
                new = (field, known)
        return new

    base, known = run("start", state, moved["start"][1:], source, state)
    image, known = run("plain", base, known, None)
    dots = run("dots", image, known, None, base, image)
    base, image = (lax.ppermute(a, "wet", back) for a in (base, image))
    dots = jnp.broadcast_to(dots[None], (wet * trc, 1, block))
    dots = lax.all_to_all(dots, ("wet", "trc"), 0, 0)
    out = pl.pallas_call(
        finish_kernel,
        out_shape=jax.ShapeDtypeStruct(flat, jnp.float32),
        in_specs=[VMEM] * 4,
        out_specs=VMEM,
    )(dots, home, base, image)
    return jnp.reshape(out, state_guess.shape)


def solution(mesh):
    return jax.shard_map(
        body,
        mesh=mesh,
        in_specs=(
            P("wet", "trc", None),
            P("wet", "trc", None),
            P("wet", "trc", None),
            P("wet", "trc", None, None),
            P("wet", "trc", None),
            P("wet", None),
            P("wet"),
        ),
        out_specs=P("wet", "trc", None),
        check_vma=False,
    )
```
